512 devices in a mesh: slab: 4 (over x_hi, core), energy: 128 (over y, z, x_lo).
Axes of the slice: x: 4 (x_hi: 2, x_lo: 2; x = x_hi * 2 + x_lo), y: 4, z: 16, core: 2. Of those that a mesh axis runs over, the one named last changes fastest.
Arguments:
- onsite: float32 [4, 384], P('slab'), may hold values from -1 to 1
- hopping: float32 [4, 384, 384], P('slab'), may hold values from -0.09 to 0.09, as said below
- separator_hamiltonian: float32 [128, 128], replicated, may hold values from -1 to 1, as said below
- coupling: float32 [4, 128], P('slab'), may hold values from 0.3 to 0.8
- bound_rows: int32 [4, 128], P('slab'), may hold values from 0 to 383, as said below
- old_sigma: float32 [2, 128, 4, 384, 384], P(None, 'energy', 'slab'), may hold values from -0.125 to 0.125
- phonon_vertex: float32 [4, 384, 384], P('slab'), may hold values from -0.3125 to 0.3125
- mode_steps: int32 [2], replicated, may hold values from 1 to 2, as said below
- mode_weights: float32 [2, 2], replicated, may hold values from 0.3 to 3
Outputs:
- new_sigma: float32 [2, 128, 4, 384, 384], P(None, 'energy', 'slab')
The draws below stay inside these ranges and needn't reach their ends.
Inputs may be any that keep to these rules, and one draw needn't show every extreme that they name: Each slab's hopping block is symmetric with a zero diagonal. `separator_hamiltonian`: symmetric. `bound_rows`: each slab's 128 entries are distinct and ascending and include the slab's first and last orbital. `mode_steps`: the 2 modes have distinct steps.
All inputs are finite; a program needn't handle non-finite values.
Results may differ from the reference program's by a relative error of at most 0.0001.
Values sent between devices are 32-bit elements; how exact they have to be, the bound alone decides.
A program may use at most 192 MiB of HBM per device.

```python
import math
import jax
import jax.numpy as jnp
from jax import lax

SLAB = 384
SEP = 128
ITERS = 3
MODES = 2
SLABS = 4
ENERGIES = 128


def symmetric_block(key, count, order_size, scale):
    raw = jnp.clip(jax.random.normal(key, (count, order_size, order_size), jnp.float32), -4.0, 4.0)
    mirrored = (raw + jnp.swapaxes(raw, -1, -2)) * (scale / math.sqrt(2.0))
    return mirrored * (1.0 - jnp.eye(order_size, dtype=jnp.float32))


def draw_hopping(key, part):
    return symmetric_block(jax.random.fold_in(key, 11), SLABS, SLAB, 0.015)


def draw_separator_hamiltonian(key, part):
    offdiag = symmetric_block(jax.random.fold_in(key, 23), 1, SEP, 0.015)[0]
    levels = jax.random.uniform(jax.random.fold_in(key, 29), (SEP,), jnp.float32, -1.0, 1.0)
    return offdiag + jnp.diag(levels)


def draw_bound_rows(key, part):
    keys = jax.random.split(jax.random.fold_in(key, 37), SLABS)

    def one_slab(slab_key):
        inner = jax.random.permutation(slab_key, SLAB - 2).astype(jnp.int32) + 1
        chosen = jnp.concatenate([jnp.zeros((1,), jnp.int32), inner[:SEP - 2], jnp.full((1,), SLAB - 1, jnp.int32)])
        return jnp.sort(chosen)
    return jax.vmap(one_slab)(keys).astype(jnp.int32)


def draw_mode_steps(key, part):
    return (jax.random.permutation(jax.random.fold_in(key, 41), MODES).astype(jnp.int32) + 1).astype(jnp.int32)


def steps_of(key, extent, shards, least, top_value):
    factor_of = 1.0
    for axis_at, parts in shards:
        heights = jax.random.uniform(jax.random.fold_in(jax.random.fold_in(key, 6), axis_at), (parts,), jnp.float32, least / len(shards), top_value / len(shards))
        factor_of = factor_of * jnp.repeat(jnp.exp(heights), extent[axis_at] // parts).reshape((-1,) + (1,) * (len(extent) - 1 - axis_at))
    return factor_of


def centred(key, extent, spread, limit, cuts=(), kind=jnp.bfloat16):
    drawn = jax.random.normal(key, extent, jnp.float32) * spread
    if len(cuts) > 0:
        drawn = steps_of(key, extent, cuts, -0.22, 0.18) * drawn
    return jnp.clip(drawn, min=-limit, max=limit).astype(kind)


def setup_inputs(seed: int = 0) -> dict:
    streams_of = jax.random.split(jax.random.key(seed), 10)
    onsite = jnp.clip(jax.random.uniform(streams_of[0], (SLABS, SLAB), jnp.float32, -1.0, 1.0) * steps_of(streams_of[0], (SLABS, SLAB), ((0, 4),), -0.4, 0.0), -1.0, 1.0)
    hopping = draw_hopping(jax.random.fold_in(streams_of[9], 71), 0)
    separator_hamiltonian = draw_separator_hamiltonian(jax.random.fold_in(streams_of[9], 71), 0)
    coupling = jnp.clip(0.3 + 0.5 * jax.random.uniform(streams_of[3], (SLABS, SEP), jnp.float32) ** steps_of(streams_of[3], (SLABS, SEP), ((0, 4),), -0.2, 0.2), 0.3, 0.8)
    bound_rows = draw_bound_rows(jax.random.fold_in(streams_of[9], 71), 0)
    old_sigma = centred(streams_of[5], (2, ENERGIES, SLABS, SLAB, SLAB), 0.008, 0.125, ((1, 128), (2, 4)), jnp.float32)
    phonon_vertex = centred(streams_of[6], (SLABS, SLAB, SLAB), SLAB ** -0.5, 0.3125, ((0, 4),), jnp.float32)
    mode_steps = draw_mode_steps(jax.random.fold_in(streams_of[9], 71), 0)
    mode_weights = jnp.clip(jnp.exp(jax.random.uniform(streams_of[8], (2, MODES), jnp.float32, math.log(0.3), math.log(3.0))), 0.3, 3.0)
    return {"onsite": onsite, "hopping": hopping, "separator_hamiltonian": separator_hamiltonian, "coupling": coupling, "bound_rows": bound_rows, "old_sigma": old_sigma, "phonon_vertex": phonon_vertex, "mode_steps": mode_steps, "mode_weights": mode_weights}


BROADENING = 1.0
LOWEST = -2.0
SPREAD = 4.0


def complex_product(former, latter):
    highest = lax.Precision.HIGHEST
    real_part = jnp.matmul(former[0], latter[0], precision=highest) - jnp.matmul(former[1], latter[1], precision=highest)
    imaginary = jnp.matmul(former[0], latter[1], precision=highest) + jnp.matmul(former[1], latter[0], precision=highest)
    return jnp.stack([real_part, imaginary])


def complex_scale(former, latter):
    real_part = former[0] * latter[0] - former[1] * latter[1]
    imaginary = former[0] * latter[1] + former[1] * latter[0]
    return jnp.stack([real_part, imaginary])


def refine(matrix):
    order_size = matrix.shape[-1]
    identity = jnp.eye(order_size, dtype=jnp.float32)
    diagonal = jnp.diagonal(matrix, axis1=-2, axis2=-1)
    magnitude = diagonal[0] * diagonal[0] + diagonal[1] * diagonal[1]
    start = jnp.stack([diagonal[0] / magnitude, -diagonal[1] / magnitude])
    first = complex_scale(complex_scale(start[..., :, None], matrix), start[..., None, :])
    estimate = 2.0 * identity * start[..., None, :] - first
    for repeat in range(ITERS - 1):
        product = complex_product(matrix, estimate)
        correction = jnp.stack([2.0 * identity - product[0], -product[1]])
        estimate = complex_product(estimate, correction)
    return estimate


def green_blocks(sigma_one, energy_value, onsite, hopping, separator_hamiltonian, coupling, bound_rows):
    order_size = hopping.shape[-1]
    identity = jnp.eye(order_size, dtype=jnp.float32)
    real_part = energy_value * identity - hopping - onsite[:, :, None] * identity - sigma_one[0]
    imaginary = BROADENING * identity - sigma_one[1]
    slab_inverse = refine(jnp.stack([real_part, imaginary]))
    picked = jnp.take_along_axis(slab_inverse, bound_rows[None, :, None, :], axis=3)
    corner = jnp.take_along_axis(picked, bound_rows[None, :, :, None], axis=2)
    weighted = corner * coupling[None, :, :, None] * coupling[None, :, None, :]
    schur = jnp.sum(weighted, axis=1)
    sep_identity = jnp.eye(separator_hamiltonian.shape[0], dtype=jnp.float32)
    separator = jnp.stack([energy_value * sep_identity - separator_hamiltonian - schur[0], BROADENING * sep_identity - schur[1]])
    separator_inverse = refine(separator)
    columns = picked * coupling[None, :, None, :]
    rows_part = jnp.take_along_axis(slab_inverse, bound_rows[None, :, :, None], axis=2) * coupling[None, :, :, None]
    middle = complex_product(columns, separator_inverse[:, None])
    return slab_inverse + complex_product(middle, rows_part)


def offset_weights(mode_steps, mode_weights):
    distances = jnp.arange(1, 3, dtype=jnp.int32)
    matched = (mode_steps[None, :] == distances[:, None]).astype(jnp.float32)
    absorb = jnp.sum(matched * mode_weights[0][None, :], axis=1)
    emit = jnp.sum(matched * mode_weights[1][None, :], axis=1)
    return absorb, emit


def reference(onsite, hopping, separator_hamiltonian, coupling, bound_rows, old_sigma, phonon_vertex, mode_steps, mode_weights):
    energy_count = old_sigma.shape[1]

    def one_energy(packed):
        sigma_one, energy_index = packed
        energy_value = LOWEST + SPREAD * (energy_index.astype(jnp.float32) + 0.5) / energy_count
        return green_blocks(sigma_one, energy_value, onsite, hopping, separator_hamiltonian, coupling, bound_rows)

    greens = lax.map(one_energy, (jnp.moveaxis(old_sigma, 1, 0), jnp.arange(energy_count, dtype=jnp.int32)))
    absorb, emit = offset_weights(mode_steps, mode_weights)
    mixed = jnp.zeros_like(greens)
    for distance in (1, 2):
        lower = jnp.concatenate([jnp.zeros_like(greens[:distance]), greens[:-distance]], axis=0)
        upper = jnp.concatenate([greens[distance:], jnp.zeros_like(greens[:distance])], axis=0)
        mixed = mixed + absorb[distance - 1] * lower + emit[distance - 1] * upper

    def sandwich(block):
        highest = lax.Precision.HIGHEST
        inner = jnp.matmul(phonon_vertex[None], block, precision=highest)
        return jnp.matmul(inner, jnp.swapaxes(phonon_vertex, -1, -2)[None], precision=highest)

    dressed = lax.map(sandwich, mixed)
    return jnp.moveaxis(dressed, 0, 1)
```

```python
import functools

import jax
import jax.numpy as jnp
from jax import lax
from jax.experimental import pallas as pl
from jax.experimental.pallas import tpu as pltpu
from jax.sharding import PartitionSpec as P

BROADENING = 1.0
LOWEST = -2.0
SPREAD = 4.0
CHUNK = 32
WINDOW = 3
LAG = 2
F32 = jnp.float32
BF16 = jnp.bfloat16


def split(x):
    high = x.astype(BF16)
    return high, (x - high.astype(F32)).astype(BF16)


def dot(x, y):
    return jnp.dot(x, y, preferred_element_type=F32)


def dot3(xh, xl, yh, yl):
    return dot(xh, yh) + dot(xh, yl) + dot(xl, yh)


def rot(p, b):
    r = (p.shape[1] - 2 * b) // 2
    parts = [-p[:, b : 2 * b], p[:, :b]]
    if r:
        parts += [-p[:, 2 * b + r :], p[:, 2 * b : 2 * b + r]]
    return jnp.concatenate(parts, axis=1)


def rot_rest(p):
    r = p.shape[1] // 2
    return jnp.concatenate([-p[:, r:], p[:, :r]], axis=1)


def iota(shape, axis):
    return lax.broadcasted_iota(jnp.int32, shape, axis)


def kernel(
    onsite_ref,
    hop_ref,
    ham_ref,
    cpl_ref,
    bound_ref,
    sigma_ref,
    vertex_ref,
    steps_ref,
    weights_ref,
    out_ref,
    khl,
    rhs,
    k2l,
    k4r,
    yv,
    yl,
    av,
    al,
    rr,
    vp,
    vt,
    q,
    acc,
    s_ref,
    r1_ref,
    h2_ref,
    r2_ref,
    f_ref,
    g_ref,
    x_ref,
    one_ref,
    sum_ref,
    got_ref,
    schur_send,
    schur_recv,
    x_send,
    x_recv,
    one_send,
    one_recv,
    sum_send,
    sum_recv,
):
    n = hop_ref.shape[-1]
    b = ham_ref.shape[0]
    r = n - b
    slab = lax.axis_index("slab")
    e = lax.axis_index("energy")
    energies = lax.axis_size("energy")
    core = lax.rem(slab, 2)
    other_core = slab + 1 - 2 * core
    other_chip = lax.rem(slab + 2, 4)
    odd = lax.rem(e, 2)
    pair = e + 1 - 2 * odd
    one_to = lax.rem(e - 2 + 4 * odd + energies, energies)
    sum_to = lax.rem(e + 2 - 4 * odd + energies, energies)

    barrier = pltpu.get_barrier_semaphore()
    for target in (
        {"slab": other_core},
        {"slab": other_chip},
        {"energy": pair},
        {"energy": one_to},
        {"energy": sum_to},
    ):
        pl.semaphore_signal(barrier, inc=1, device_id=target, device_id_type=pl.DeviceIdType.MESH)

    def remote(src, dst, send, recv, target):
        return pltpu.make_async_remote_copy(
            src_ref=src,
            dst_ref=dst,
            send_sem=send,
            recv_sem=recv,
            device_id=target,
            device_id_type=pl.DeviceIdType.MESH,
        )

    energy_value = LOWEST + SPREAD * (e.astype(F32) + 0.5) / energies

    eye_b = iota((b, b), 0) == iota((b, b), 1)
    bound_row = bound_ref[...]
    bound_col = jnp.sum(jnp.where(eye_b, bound_row, 0), axis=1, keepdims=True)
    here = iota((b, n), 1)
    count = jnp.sum(jnp.where(bound_col < here, 1, 0), axis=0, keepdims=True)
    is_bound = jnp.sum(jnp.where(bound_col == here, 1, 0), axis=0, keepdims=True)
    at = iota((1, n), 1)
    pos_row = jnp.where(is_bound > 0, count, b + at - count)
    here = iota((n, b), 0)
    count = jnp.sum(jnp.where(bound_row < here, 1, 0), axis=1, keepdims=True)
    is_bound = jnp.sum(jnp.where(bound_row == here, 1, 0), axis=1, keepdims=True)
    at = iota((n, 1), 0)
    pos_col = jnp.where(is_bound > 0, count, b + at - count)
    perm_mask = iota((n, n), 0) == pos_row
    perm = jnp.where(perm_mask, 1.0, 0.0).astype(BF16)
    perm_t = jnp.where(iota((n, n), 1) == pos_col, 1.0, 0.0).astype(BF16)

    eye = iota((n, n), 0) == iota((n, n), 1)
    sr = hop_ref[0] + sigma_ref[0, 0, 0]
    si = sigma_ref[1, 0, 0]
    dr = energy_value - onsite_ref[...] - jnp.sum(jnp.where(eye, sr, 0.0), axis=0, keepdims=True)
    di = BROADENING - jnp.sum(jnp.where(eye, si, 0.0), axis=0, keepdims=True)
    magnitude = dr * dr + di * di
    dr, di = dr / magnitude, -di / magnitude
    nr = jnp.where(eye, 0.0, -sr)
    ni = jnp.where(eye, 0.0, -si)
    krh, krl = split(nr * dr - ni * di)
    kih, kil = split(nr * di + ni * dr)
    moved = dot(perm, jnp.concatenate([krh, kih, krl, kil], axis=1)).astype(BF16)
    krh, kih, krl, kil = (dot(moved[:, i * n : (i + 1) * n], perm_t).astype(BF16) for i in range(4))
    dr_col = jnp.sum(jnp.where(perm_mask, dr, 0.0), axis=1, keepdims=True)
    di_col = jnp.sum(jnp.where(perm_mask, di, 0.0), axis=1, keepdims=True)

    def ordered(re, im):
        return jnp.concatenate([re[:, :b], im[:, :b], re[:, b:], im[:, b:]], axis=1)

    def store_rhs(ref, at, p, turned, columns):
        ref[at, 0:b, columns] = p[:b]
        ref[at, b : 2 * b, columns] = turned[:b]
        ref[at, 2 * b : 2 * b + r, columns] = p[b:]
        ref[at, 2 * b + r :, columns] = turned[b:]

    whole = slice(0, 2 * n)
    first = slice(0, 2 * b)
    rest = slice(2 * b, 2 * n)
    for i, p in enumerate((ordered(krh, kih), ordered(krl, kil))):
        khl[i] = p
        store_rhs(rhs, i, p, rot(p, b), whole)

    p = dot3(khl[0], khl[1], rhs[0], rhs[1])
    yv[...] = p
    for i, part in enumerate(split(p)):
        k2l[i] = part
        store_rhs(rhs, i, part, rot(part, b), whole)

    def identity(start, rows):
        row = iota((rows, 2 * n), 0) + start
        column = iota((rows, 2 * n), 1)
        orbital = jnp.where(column < b, column, jnp.where((column >= 2 * b) & (column < 2 * b + r), column - b, -1))
        return jnp.where(row == orbital, 1.0, 0.0)

    def y_rows(start, rows):
        at = slice(start, start + rows)
        k3 = dot3(khl[0, at], khl[1, at], rhs[0], rhs[1])
        u = identity(start, rows) - khl[0, at].astype(F32) - khl[1, at].astype(F32) + yv[at] - k3
        y = dr_col[at] * u + di_col[at] * rot(u, b)
        yv[at] = y
        for i, part in enumerate(split(y)):
            yl[i, at] = part

    def k4_columns(columns, turn):
        p = dot3(k2l[0], k2l[1], rhs[0, :, columns], rhs[1, :, columns])
        for i, part in enumerate(split(p)):
            store_rhs(k4r, i, part, turn(part), columns)

    y_rows(0, b)
    k4_columns(first, lambda part: rot(part, b))
    corner = yv[:b, first] + dot3(yl[0, :b], yl[1, :b], k4r[0, :, first], k4r[1, :, first])
    c_row = cpl_ref[...]
    c_col = jnp.sum(jnp.where(eye_b, c_row, 0.0), axis=1, keepdims=True)
    c_both = c_col * c_row
    s_ref[0] = corner[:, :b] * c_both
    s_ref[1] = corner[:, b:] * c_both

    pl.semaphore_wait(barrier, 5)
    step1 = remote(s_ref.at[1 - core], r1_ref, schur_send.at[0], schur_recv.at[0], {"slab": other_core})
    step1.start()
    y_rows(b, r)
    step1.wait()
    h2_ref[...] = s_ref[core] + r1_ref[...]
    step2 = remote(h2_ref, r2_ref, schur_send.at[1], schur_recv.at[1], {"slab": other_chip})
    step2.start()

    k4_columns(rest, rot_rest)
    a = yv[...] + dot3(yl[0], yl[1], k4r[0], k4r[1])
    av[...] = a
    for i, part in enumerate(split(a[:, first])):
        al[i] = part
    for i, part in enumerate(split(a[:b])):
        rr[i, :b] = part
        rr[i, b:] = rot(part, b)

    step2.wait()
    f_ref[core] = h2_ref[...] + r2_ref[...]
    step3 = remote(f_ref.at[core], f_ref.at[core], schur_send.at[2], schur_recv.at[2], {"slab": other_core})
    step3.start()
    for i, part in enumerate(split(vertex_ref[0])):
        v = dot(part, perm_t)
        vp[i] = v.astype(BF16)
        vt[i] = v.T.astype(BF16)
    step3.wait()

    tr = jnp.where(eye_b, 0.0, -ham_ref[...] - f_ref[0])
    ti = jnp.where(eye_b, 0.0, -f_ref[1])
    diag_r = jnp.where(eye_b, energy_value - ham_ref[...] - f_ref[0], 0.0)
    diag_i = jnp.where(eye_b, BROADENING - f_ref[1], 0.0)

    def reciprocal(axis):
        zr = jnp.sum(diag_r, axis=axis, keepdims=True)
        zi = jnp.sum(diag_i, axis=axis, keepdims=True)
        size = zr * zr + zi * zi
        return zr / size, -zi / size

    er, ei = reciprocal(0)
    er_col, ei_col = reciprocal(1)
    k = jnp.concatenate([tr * er - ti * ei, tr * ei + ti * er], axis=1)

    def turned(parts):
        return [jnp.concatenate([part, rot(part, b)], axis=0) for part in parts]

    one = jnp.where(iota((b, 2 * b), 0) == iota((b, 2 * b), 1), 1.0, 0.0)
    kl = split(k)
    k2 = dot3(*kl, *turned(kl))
    k2s = split(k2)
    k2t = turned(k2s)
    k3 = dot3(*kl, *k2t)
    k4 = dot3(*k2s, *k2t)
    u = one - k + k2 - k3
    u = er_col * u + ei_col * rot(u, b)
    t = u + dot3(*split(u), *turned(split(k4)))
    t = t * jnp.concatenate([c_both, c_both], axis=1)
    th, tl = turned(split(t))

    w = [[jnp.float32(0.0), jnp.float32(0.0)], [jnp.float32(0.0), jnp.float32(0.0)]]
    for way in range(2):
        for d in range(2):
            for m in range(2):
                w[way][d] = w[way][d] + jnp.where(steps_ref[m] == d + 1, weights_ref[way, m], 0.0)
    is_odd = odd == 1
    w_sum_own = jnp.where(is_odd, w[1][1], w[0][1])
    w_sum_pair = jnp.where(is_odd, w[1][0], w[0][0])
    w_pair = jnp.where(is_odd, w[0][0], w[1][0])
    one_from = e + 2 - 4 * odd
    sum_from = e - 2 + 4 * odd
    has_one = (one_from >= 0) & (one_from < energies)
    has_sum = (sum_from >= 0) & (sum_from < energies)
    w_one = jnp.where(is_odd, w[0][1], w[1][1])

    chunks = n // CHUNK
    started = []

    def x_copy(c):
        at = pl.ds(c * CHUNK, CHUNK)
        return remote(g_ref.at[at], x_ref.at[at], x_send.at[c], x_recv.at[c], {"energy": pair})

    def one_copy(c):
        at = pl.ds(c * CHUNK, CHUNK)
        return remote(g_ref.at[at], one_ref.at[at], one_send.at[c], one_recv.at[c], {"energy": one_to})

    def sum_copy(c):
        at = pl.ds(c * CHUNK, CHUNK)
        return remote(sum_ref.at[at], got_ref.at[at], sum_send.at[c], sum_recv.at[c], {"energy": sum_to})

    def send(c):
        x_copy(c).start()
        one_copy(c).start()

    for c in range(chunks):
        at = slice(c * CHUNK, (c + 1) * CHUNK)
        middle = dot3(al[0, at], al[1, at], th, tl)
        g_ref[at] = av[at] + dot3(*split(middle), rr[0], rr[1])
        if c < WINDOW:
            send(c)

    def mix(c):
        one_copy(c).wait_recv()
        sum_copy(c).wait_recv()
        at = slice(c * CHUNK, (c + 1) * CHUNK)
        mixed = w_pair * x_ref[at]
        mixed = mixed + jnp.where(has_one, w_one * one_ref[at], 0.0)
        mixed = mixed + jnp.where(has_sum, got_ref[at], 0.0)
        stacked = jnp.concatenate(
            [
                jnp.concatenate([mixed[:, :b], mixed[:, 2 * b : 2 * b + r]], axis=1),
                jnp.concatenate([mixed[:, b : 2 * b], mixed[:, 2 * b + r :]], axis=1),
            ],
            axis=0,
        )
        dressed = dot3(*split(stacked), vt[0], vt[1])
        for i, part in enumerate(split(dressed)):
            q[i, at, :n] = part[:CHUNK]
            q[i, at, n:] = part[CHUNK:]
        if (c + 1) * CHUNK == n - b:
            early = slice(0, n - b)
            acc[...] = dot3(vp[0, :, early], vp[1, :, early], q[0, early], q[1, early])

    for c in range(chunks + LAG):
        if c < chunks:
            x_copy(c).wait_recv()
            at = slice(c * CHUNK, (c + 1) * CHUNK)
            sum_ref[at] = w_sum_own * g_ref[at] + w_sum_pair * x_ref[at]
            sum_copy(c).start()
            if c + WINDOW < chunks:
                send(c + WINDOW)
        if c >= LAG:
            mix(c - LAG)

    late = slice(n - b, n)
    result = acc[...] + dot3(vp[0, :, late], vp[1, :, late], q[0, late], q[1, late])
    out_ref[0, 0, 0] = result[:, :n]
    out_ref[1, 0, 0] = result[:, n:]
    for c in range(chunks):
        x_copy(c).wait_send()
        one_copy(c).wait_send()
        sum_copy(c).wait_send()


def per_device(*arrays):
    n = arrays[1].shape[-1]
    b = arrays[2].shape[0]
    chunks = n // CHUNK
    vmem = pl.BlockSpec(memory_space=pltpu.VMEM)
    smem = pl.BlockSpec(memory_space=pltpu.SMEM)
    dma = pltpu.SemaphoreType.DMA
    return pl.pallas_call(
        kernel,
        out_shape=jax.ShapeDtypeStruct(arrays[5].shape, F32),
        in_specs=[vmem] * 7 + [smem] * 2,
        out_specs=vmem,
        scratch_shapes=[
            pltpu.VMEM((2, n, 2 * n), BF16),
            pltpu.VMEM((2, 2 * n, 2 * n), BF16),
            pltpu.VMEM((2, n, 2 * n), BF16),
            pltpu.VMEM((2, 2 * n, 2 * n), BF16),
            pltpu.VMEM((n, 2 * n), F32),
            pltpu.VMEM((2, n, 2 * n), BF16),
            pltpu.VMEM((n, 2 * n), F32),
            pltpu.VMEM((2, n, 2 * b), BF16),
            pltpu.VMEM((2, 2 * b, 2 * n), BF16),
            pltpu.VMEM((2, n, n), BF16),
            pltpu.VMEM((2, n, n), BF16),
            pltpu.VMEM((2, n, 2 * n), BF16),
            pltpu.VMEM((n, 2 * n), F32),
            pltpu.VMEM((2, b, b), F32),
            pltpu.VMEM((b, b), F32),
            pltpu.VMEM((b, b), F32),
            pltpu.VMEM((b, b), F32),
            pltpu.VMEM((2, b, b), F32),
            pltpu.VMEM((n, 2 * n), F32),
            pltpu.VMEM((n, 2 * n), F32),
            pltpu.VMEM((n, 2 * n), F32),
            pltpu.VMEM((n, 2 * n), F32),
            pltpu.VMEM((n, 2 * n), F32),
            dma((3,)),
            dma((3,)),
            dma((chunks,)),
            dma((chunks,)),
            dma((chunks,)),
            dma((chunks,)),
            dma((chunks,)),
            dma((chunks,)),
        ],
        compiler_params=pltpu.CompilerParams(
            collective_id=0, has_side_effects=True, vmem_limit_bytes=52 * 2**20
        ),
    )(*arrays)


def solution(mesh):
    placed = (
        P("slab", None),
        P("slab", None, None),
        P(),
        P("slab", None),
        P("slab", None),
        P(None, "energy", "slab", None, None),
        P("slab", None, None),
        P(),
        P(),
    )
    return jax.shard_map(
        per_device,
        mesh=mesh,
        in_specs=placed,
        out_specs=P(None, "energy", "slab", None, None),
        check_vma=False,
    )
```

```python
import functools

import jax
import jax.numpy as jnp
from jax import lax
from jax.experimental import pallas as pl
from jax.experimental.pallas import tpu as pltpu
from jax.sharding import PartitionSpec as P

BROADENING = 1.0
LOWEST = -2.0
SPREAD = 4.0
CHUNK = 32
WINDOW = 3
LAG = 2
GROUPS = (32, 96, 256)
F32 = jnp.float32
BF16 = jnp.bfloat16


def split(x):
    high = x.astype(BF16)
    return high, (x - high.astype(F32)).astype(BF16)


def dot(x, y):
    return jnp.dot(x, y, preferred_element_type=F32)


def dot3(xh, xl, yh, yl):
    return dot(xh, yh) + dot(xh, yl) + dot(xl, yh)


def rot(p, b):
    r = (p.shape[1] - 2 * b) // 2
    parts = [-p[:, b : 2 * b], p[:, :b]]
    if r:
        parts += [-p[:, 2 * b + r :], p[:, 2 * b : 2 * b + r]]
    return jnp.concatenate(parts, axis=1)


def rot_rest(p):
    r = p.shape[1] // 2
    return jnp.concatenate([-p[:, r:], p[:, :r]], axis=1)


def iota(shape, axis):
    return lax.broadcasted_iota(jnp.int32, shape, axis)


def kernel(
    onsite_in,
    hop_in,
    ham_in,
    cpl_in,
    bound_in,
    sigma_in,
    vertex_in,
    steps_ref,
    weights_ref,
    out_ref,
    onsite_ref,
    hop_ref,
    ham_ref,
    cpl_ref,
    bound_ref,
    sigma_ref,
    vertex_ref,
    res_ref,
    in_sem,
    out_sem,
    khl,
    rhs,
    k2l,
    k4r,
    yv,
    yl,
    av,
    al,
    rr,
    vp,
    vt,
    q,
    acc,
    th_ref,
    s_ref,
    r1_ref,
    h2_ref,
    r2_ref,
    f_ref,
    g_ref,
    x_ref,
    one_ref,
    sum_ref,
    got_ref,
    schur_send,
    schur_recv,
    x_send,
    x_recv,
    one_send,
    one_recv,
    sum_send,
    sum_recv,
):
    n = hop_ref.shape[-1]
    b = ham_ref.shape[0]
    r = n - b
    slab = lax.axis_index("slab")
    e = lax.axis_index("energy")
    energies = lax.axis_size("energy")
    core = lax.rem(slab, 2)
    other_core = slab + 1 - 2 * core
    other_chip = lax.rem(slab + 2, 4)
    odd = lax.rem(e, 2)
    pair = e + 1 - 2 * odd
    one_to = lax.rem(e - 2 + 4 * odd + energies, energies)
    sum_to = lax.rem(e + 2 - 4 * odd + energies, energies)

    loads = [
        pltpu.make_async_copy(src, dst, in_sem.at[i])
        for i, (src, dst) in enumerate(
            (
                (bound_in, bound_ref),
                (sigma_in, sigma_ref),
                (hop_in, hop_ref),
                (onsite_in, onsite_ref),
                (cpl_in, cpl_ref),
                (ham_in, ham_ref),
                (vertex_in, vertex_ref),
            )
        )
    ]
    for load in loads[:5]:
        load.start()
    barrier = pltpu.get_barrier_semaphore()
    for target in (
        {"slab": other_core},
        {"slab": other_chip},
        {"energy": pair},
        {"energy": one_to},
        {"energy": sum_to},
    ):
        pl.semaphore_signal(barrier, inc=1, device_id=target, device_id_type=pl.DeviceIdType.MESH)

    def remote(src, dst, send, recv, target):
        return pltpu.make_async_remote_copy(
            src_ref=src,
            dst_ref=dst,
            send_sem=send,
            recv_sem=recv,
            device_id=target,
            device_id_type=pl.DeviceIdType.MESH,
        )

    def apart(work):
        pl.when(slab >= 0)(work)

    energy_value = LOWEST + SPREAD * (e.astype(F32) + 0.5) / energies

    loads[0].wait()
    eye_b = iota((b, b), 0) == iota((b, b), 1)
    bound_row = bound_ref[...]
    bound_col = jnp.sum(jnp.where(eye_b, bound_row, 0), axis=1, keepdims=True)
    here = iota((b, n), 1)
    count = jnp.sum(jnp.where(bound_col < here, 1, 0), axis=0, keepdims=True)
    is_bound = jnp.sum(jnp.where(bound_col == here, 1, 0), axis=0, keepdims=True)
    at = iota((1, n), 1)
    pos_row = jnp.where(is_bound > 0, count, b + at - count)
    here = iota((n, b), 0)
    count = jnp.sum(jnp.where(bound_row < here, 1, 0), axis=1, keepdims=True)
    is_bound = jnp.sum(jnp.where(bound_row == here, 1, 0), axis=1, keepdims=True)
    at = iota((n, 1), 0)
    pos_col = jnp.where(is_bound > 0, count, b + at - count)
    perm_mask = iota((n, n), 0) == pos_row
    perm = jnp.where(perm_mask, 1.0, 0.0).astype(BF16)
    perm_t = jnp.where(iota((n, n), 1) == pos_col, 1.0, 0.0).astype(BF16)

    for load in loads[1:4]:
        load.wait()
    for load in loads[5:]:
        load.start()
    eye = iota((n, n), 0) == iota((n, n), 1)
    sr = hop_ref[0] + sigma_ref[0, 0, 0]
    si = sigma_ref[1, 0, 0]
    dr = energy_value - onsite_ref[...] - jnp.sum(jnp.where(eye, sr, 0.0), axis=0, keepdims=True)
    di = BROADENING - jnp.sum(jnp.where(eye, si, 0.0), axis=0, keepdims=True)
    magnitude = dr * dr + di * di
    dr, di = dr / magnitude, -di / magnitude
    nr = jnp.where(eye, 0.0, -sr)
    ni = jnp.where(eye, 0.0, -si)
    krh, krl = split(nr * dr - ni * di)
    kih, kil = split(nr * di + ni * dr)
    moved = dot(perm, jnp.concatenate([krh, kih, krl, kil], axis=1)).astype(BF16)
    krh, kih, krl, kil = (dot(moved[:, i * n : (i + 1) * n], perm_t).astype(BF16) for i in range(4))
    rows = iota((8, n), 0)
    pieces = jnp.zeros((8, n), F32)
    for i, d in enumerate((dr, di)):
        for j in range(3):
            part = d.astype(BF16).astype(F32)
            pieces = jnp.where(rows == 3 * i + j, part, pieces)
            d = d - part
    pieces = dot(pieces.astype(BF16), perm_t).T
    dr_col = pieces[:, 0:1] + pieces[:, 1:2] + pieces[:, 2:3]
    di_col = pieces[:, 3:4] + pieces[:, 4:5] + pieces[:, 5:6]

    def ordered(re, im):
        return jnp.concatenate([re[:, :b], im[:, :b], re[:, b:], im[:, b:]], axis=1)

    def store_rhs(ref, at, p, turned, columns):
        ref[at, 0:b, columns] = p[:b]
        ref[at, b : 2 * b, columns] = turned[:b]
        ref[at, 2 * b : 2 * b + r, columns] = p[b:]
        ref[at, 2 * b + r :, columns] = turned[b:]

    whole = slice(0, 2 * n)
    first = slice(0, 2 * b)
    rest = slice(2 * b, 2 * n)
    for i, p in enumerate((ordered(krh, kih), ordered(krl, kil))):
        khl[i] = p
        store_rhs(rhs, i, p, rot(p, b), whole)

    p = dot3(khl[0], khl[1], rhs[0], rhs[1])
    yv[...] = p
    for i, part in enumerate(split(p)):
        k2l[i] = part
        store_rhs(rhs, i, part, rot(part, b), whole)

    def identity(start, rows):
        row = iota((rows, 2 * n), 0) + start
        column = iota((rows, 2 * n), 1)
        orbital = jnp.where(column < b, column, jnp.where((column >= 2 * b) & (column < 2 * b + r), column - b, -1))
        return jnp.where(row == orbital, 1.0, 0.0)

    def y_rows(start, rows):
        at = slice(start, start + rows)
        k3 = dot3(khl[0, at], khl[1, at], rhs[0], rhs[1])
        u = identity(start, rows) - khl[0, at].astype(F32) - khl[1, at].astype(F32) + yv[at] - k3
        y = dr_col[at] * u + di_col[at] * rot(u, b)
        yv[at] = y
        for i, part in enumerate(split(y)):
            yl[i, at] = part

    def k4_columns(columns, turn):
        p = dot3(k2l[0], k2l[1], rhs[0, :, columns], rhs[1, :, columns])
        for i, part in enumerate(split(p)):
            store_rhs(k4r, i, part, turn(part), columns)

    y_rows(0, b)
    k4_columns(first, lambda part: rot(part, b))
    corner = yv[:b, first] + dot3(yl[0, :b], yl[1, :b], k4r[0, :, first], k4r[1, :, first])
    loads[4].wait()
    c_row = cpl_ref[...]
    c_col = jnp.sum(jnp.where(eye_b, c_row, 0.0), axis=1, keepdims=True)
    c_both = c_col * c_row
    s_ref[0] = corner[:, :b] * c_both
    s_ref[1] = corner[:, b:] * c_both

    pl.semaphore_wait(barrier, 5)
    step1 = remote(s_ref.at[1 - core], r1_ref, schur_send.at[0], schur_recv.at[0], {"slab": other_core})
    step1.start()
    apart(lambda: y_rows(b, r))
    step1.wait()
    h2_ref[...] = s_ref[core] + r1_ref[...]
    step2 = remote(h2_ref, r2_ref, schur_send.at[1], schur_recv.at[1], {"slab": other_chip})
    step2.start()

    def finish_inverse():
        k4_columns(rest, rot_rest)
        a = yv[...] + dot3(yl[0], yl[1], k4r[0], k4r[1])
        av[...] = a
        for i, part in enumerate(split(a[:, first])):
            al[i] = part
        for i, part in enumerate(split(a[:b])):
            rr[i, :b] = part
            rr[i, b:] = rot(part, b)

    apart(finish_inverse)

    step2.wait()
    f_ref[core] = h2_ref[...] + r2_ref[...]
    step3 = remote(f_ref.at[core], f_ref.at[core], schur_send.at[2], schur_recv.at[2], {"slab": other_core})
    step3.start()
    loads[5].wait()
    loads[6].wait()

    def order_vertex():
        for i, part in enumerate(split(vertex_ref[0])):
            v = dot(part, perm_t)
            vp[i] = v.astype(BF16)
            vt[i] = v.T.astype(BF16)

    apart(order_vertex)
    step3.wait()

    tr = jnp.where(eye_b, 0.0, -ham_ref[...] - f_ref[0])
    ti = jnp.where(eye_b, 0.0, -f_ref[1])
    diag_r = jnp.where(eye_b, energy_value - ham_ref[...] - f_ref[0], 0.0)
    diag_i = jnp.where(eye_b, BROADENING - f_ref[1], 0.0)

    def reciprocal(axis):
        zr = jnp.sum(diag_r, axis=axis, keepdims=True)
        zi = jnp.sum(diag_i, axis=axis, keepdims=True)
        size = zr * zr + zi * zi
        return zr / size, -zi / size

    er, ei = reciprocal(0)
    er_col, ei_col = reciprocal(1)
    k = jnp.concatenate([tr * er - ti * ei, tr * ei + ti * er], axis=1)

    def turned(parts):
        return [jnp.concatenate([part, rot(part, b)], axis=0) for part in parts]

    one = jnp.where(iota((b, 2 * b), 0) == iota((b, 2 * b), 1), 1.0, 0.0)
    kl = split(k)
    k2 = dot3(*kl, *turned(kl))
    k2s = split(k2)
    k2t = turned(k2s)
    k3 = dot3(*kl, *k2t)
    k4 = dot3(*k2s, *k2t)
    u = one - k + k2 - k3
    u = er_col * u + ei_col * rot(u, b)
    t = u + dot3(*split(u), *turned(split(k4)))
    t = t * jnp.concatenate([c_both, c_both], axis=1)
    th, tl = turned(split(t))

    w = [[jnp.float32(0.0), jnp.float32(0.0)], [jnp.float32(0.0), jnp.float32(0.0)]]
    for way in range(2):
        for d in range(2):
            for m in range(2):
                w[way][d] = w[way][d] + jnp.where(steps_ref[m] == d + 1, weights_ref[way, m], 0.0)
    is_odd = odd == 1
    w_sum_own = jnp.where(is_odd, w[1][1], w[0][1])
    w_sum_pair = jnp.where(is_odd, w[1][0], w[0][0])
    w_pair = jnp.where(is_odd, w[0][0], w[1][0])
    one_from = e + 2 - 4 * odd
    sum_from = e - 2 + 4 * odd
    has_one = (one_from >= 0) & (one_from < energies)
    has_sum = (sum_from >= 0) & (sum_from < energies)
    w_one = jnp.where(is_odd, w[0][1], w[1][1])

    chunks = n // CHUNK
    started = []

    def x_copy(c):
        at = pl.ds(c * CHUNK, CHUNK)
        return remote(g_ref.at[at], x_ref.at[at], x_send.at[c], x_recv.at[c], {"energy": pair})

    def one_copy(c):
        at = pl.ds(c * CHUNK, CHUNK)
        return remote(g_ref.at[at], one_ref.at[at], one_send.at[c], one_recv.at[c], {"energy": one_to})

    def sum_copy(c):
        at = pl.ds(c * CHUNK, CHUNK)
        return remote(sum_ref.at[at], got_ref.at[at], sum_send.at[c], sum_recv.at[c], {"energy": sum_to})

    def send(c):
        x_copy(c).start()
        one_copy(c).start()

    th_ref[0], th_ref[1] = th, tl

    def greens(start, rows):
        at = slice(start, start + rows)
        middle = dot3(al[0, at], al[1, at], th_ref[0], th_ref[1])
        g_ref[at] = av[at] + dot3(*split(middle), rr[0], rr[1])

    start = 0
    for rows in GROUPS:
        apart(functools.partial(greens, start, rows))
        for c in range(start // CHUNK, min((start + rows) // CHUNK, WINDOW)):
            send(c)
        start += rows

    def mix(c):
        at = slice(c * CHUNK, (c + 1) * CHUNK)
        mixed = w_pair * x_ref[at]
        mixed = mixed + jnp.where(has_one, w_one * one_ref[at], 0.0)
        mixed = mixed + jnp.where(has_sum, got_ref[at], 0.0)
        stacked = jnp.concatenate(
            [
                jnp.concatenate([mixed[:, :b], mixed[:, 2 * b : 2 * b + r]], axis=1),
                jnp.concatenate([mixed[:, b : 2 * b], mixed[:, 2 * b + r :]], axis=1),
            ],
            axis=0,
        )
        dressed = dot3(*split(stacked), vt[0], vt[1])
        for i, part in enumerate(split(dressed)):
            q[i, at, :n] = part[:CHUNK]
            q[i, at, n:] = part[CHUNK:]
        if (c + 1) * CHUNK == n - b:
            early = slice(0, n - b)
            acc[...] = dot3(vp[0, :, early], vp[1, :, early], q[0, early], q[1, early])

    for c in range(chunks + LAG):
        if c < chunks:
            x_copy(c).wait_recv()
            at = slice(c * CHUNK, (c + 1) * CHUNK)
            sum_ref[at] = w_sum_own * g_ref[at] + w_sum_pair * x_ref[at]
            sum_copy(c).start()
            if c + WINDOW < chunks:
                send(c + WINDOW)
        if c >= LAG:
            one_copy(c - LAG).wait_recv()
            sum_copy(c - LAG).wait_recv()
            apart(functools.partial(mix, c - LAG))

    late = slice(n - b, n)
    stores = []
    for i in range(2):
        half = slice(i * n, (i + 1) * n)
        res_ref[i] = acc[:, half] + dot3(vp[0, :, late], vp[1, :, late], q[0, late, half], q[1, late, half])
        store = pltpu.make_async_copy(res_ref.at[i], out_ref.at[i, 0, 0], out_sem.at[i])
        store.start()
        stores.append(store)
    for c in range(chunks):
        x_copy(c).wait_send()
        one_copy(c).wait_send()
        sum_copy(c).wait_send()
    for store in stores:
        store.wait()


def per_device(*arrays):
    n = arrays[1].shape[-1]
    b = arrays[2].shape[0]
    chunks = n // CHUNK
    hbm = pl.BlockSpec(memory_space=pl.ANY)
    smem = pl.BlockSpec(memory_space=pltpu.SMEM)
    dma = pltpu.SemaphoreType.DMA
    return pl.pallas_call(
        kernel,
        out_shape=jax.ShapeDtypeStruct(arrays[5].shape, F32),
        in_specs=[hbm] * 7 + [smem] * 2,
        out_specs=hbm,
        scratch_shapes=[
            *(pltpu.VMEM(a.shape, a.dtype) for a in arrays[:7]),
            pltpu.VMEM((2, n, n), F32),
            dma((7,)),
            dma((2,)),
            pltpu.VMEM((2, n, 2 * n), BF16),
            pltpu.VMEM((2, 2 * n, 2 * n), BF16),
            pltpu.VMEM((2, n, 2 * n), BF16),
            pltpu.VMEM((2, 2 * n, 2 * n), BF16),
            pltpu.VMEM((n, 2 * n), F32),
            pltpu.VMEM((2, n, 2 * n), BF16),
            pltpu.VMEM((n, 2 * n), F32),
            pltpu.VMEM((2, n, 2 * b), BF16),
            pltpu.VMEM((2, 2 * b, 2 * n), BF16),
            pltpu.VMEM((2, n, n), BF16),
            pltpu.VMEM((2, n, n), BF16),
            pltpu.VMEM((2, n, 2 * n), BF16),
            pltpu.VMEM((n, 2 * n), F32),
            pltpu.VMEM((2, 2 * b, 2 * b), BF16),
            pltpu.VMEM((2, b, b), F32),
            pltpu.VMEM((b, b), F32),
            pltpu.VMEM((b, b), F32),
            pltpu.VMEM((b, b), F32),
            pltpu.VMEM((2, b, b), F32),
            pltpu.VMEM((n, 2 * n), F32),
            pltpu.VMEM((n, 2 * n), F32),
            pltpu.VMEM((n, 2 * n), F32),
            pltpu.VMEM((n, 2 * n), F32),
            pltpu.VMEM((n, 2 * n), F32),
            dma((3,)),
            dma((3,)),
            dma((chunks,)),
            dma((chunks,)),
            dma((chunks,)),
            dma((chunks,)),
            dma((chunks,)),
            dma((chunks,)),
        ],
        compiler_params=pltpu.CompilerParams(
            collective_id=0, has_side_effects=True, vmem_limit_bytes=60 * 2**20
        ),
    )(*arrays)


def solution(mesh):
    placed = (
        P("slab", None),
        P("slab", None, None),
        P(),
        P("slab", None),
        P("slab", None),
        P(None, "energy", "slab", None, None),
        P("slab", None, None),
        P(),
        P(),
    )
    return jax.shard_map(
        per_device,
        mesh=mesh,
        in_specs=placed,
        out_specs=P(None, "energy", "slab", None, None),
        check_vma=False,
    )
```

```python
import functools

import jax
import jax.numpy as jnp
from jax import lax
from jax.experimental import pallas as pl
from jax.experimental.pallas import tpu as pltpu
from jax.sharding import PartitionSpec as P

BROADENING = 1.0
LOWEST = -2.0
SPREAD = 4.0
CHUNK = 32
MIX = 32
ONE = 128
PART = 32
WINDOW = 3
LAG = 2
GROUPS = (32, 96, 256)
F32 = jnp.float32
BF16 = jnp.bfloat16


def split(x):
    high = x.astype(BF16)
    return high, (x - high.astype(F32)).astype(BF16)


def dot(x, y):
    return jnp.dot(x, y, preferred_element_type=F32)


def dot3(xh, xl, yh, yl):
    return dot(jnp.concatenate([xh, xh, xl], axis=1), jnp.concatenate([yh, yl, yh], axis=0))


def rot(p, b):
    r = (p.shape[1] - 2 * b) // 2
    parts = [-p[:, b : 2 * b], p[:, :b]]
    if r:
        parts += [-p[:, 2 * b + r :], p[:, 2 * b : 2 * b + r]]
    return jnp.concatenate(parts, axis=1)


def rot_rest(p):
    r = p.shape[1] // 2
    return jnp.concatenate([-p[:, r:], p[:, :r]], axis=1)


def iota(shape, axis):
    return lax.broadcasted_iota(jnp.int32, shape, axis)


def kernel(
    onsite_in,
    hop_in,
    ham_in,
    cpl_in,
    bound_in,
    sigma_in,
    vertex_in,
    steps_ref,
    weights_ref,
    out_ref,
    onsite_ref,
    hop_ref,
    ham_ref,
    cpl_ref,
    bound_ref,
    sigma_ref,
    vertex_ref,
    res_ref,
    in_sem,
    out_sem,
    khl,
    rhs,
    k2l,
    k4r,
    yv,
    yl,
    av,
    al,
    rr,
    vp,
    vt,
    q,
    acc,
    th_ref,
    s_ref,
    r1_ref,
    h2_ref,
    r2_ref,
    f_ref,
    g_ref,
    x_ref,
    one_ref,
    sum_ref,
    got_ref,
    schur_send,
    schur_recv,
    x_send,
    x_recv,
    one_send,
    one_recv,
    sum_send,
    sum_recv,
):
    n = hop_ref.shape[-1]
    b = ham_ref.shape[0]
    r = n - b
    slab = lax.axis_index("slab")
    e = lax.axis_index("energy")
    energies = lax.axis_size("energy")
    core = lax.rem(slab, 2)
    other_core = slab + 1 - 2 * core
    other_chip = lax.rem(slab + 2, 4)
    odd = lax.rem(e, 2)
    pair = e + 1 - 2 * odd
    one_to = e - 2 + 4 * odd
    sum_to = e + 2 - 4 * odd
    ahead = (one_to >= 0) & (one_to < energies)
    behind = (sum_to >= 0) & (sum_to < energies)
    one_to = lax.rem(one_to + energies, energies)
    sum_to = lax.rem(sum_to + energies, energies)

    loads = [
        pltpu.make_async_copy(src, dst, in_sem.at[i])
        for i, (src, dst) in enumerate(
            (
                (bound_in, bound_ref),
                (sigma_in, sigma_ref),
                (hop_in, hop_ref),
                (onsite_in, onsite_ref),
                (cpl_in, cpl_ref),
                (ham_in, ham_ref),
                (vertex_in, vertex_ref),
            )
        )
    ]
    for load in loads[:5]:
        load.start()
    barrier = pltpu.get_barrier_semaphore()

    def greet(target):
        pl.semaphore_signal(barrier, inc=1, device_id=target, device_id_type=pl.DeviceIdType.MESH)

    greet({"slab": other_core})
    greet({"slab": other_chip})
    greet({"energy": pair})
    pl.when(ahead)(lambda: greet({"energy": one_to}))
    pl.when(behind)(lambda: greet({"energy": sum_to}))

    def remote(src, dst, send, recv, target):
        return pltpu.make_async_remote_copy(
            src_ref=src,
            dst_ref=dst,
            send_sem=send,
            recv_sem=recv,
            device_id=target,
            device_id_type=pl.DeviceIdType.MESH,
        )

    def apart(work):
        pl.when(slab >= 0)(work)

    energy_value = LOWEST + SPREAD * (e.astype(F32) + 0.5) / energies

    loads[0].wait()
    eye_b = iota((b, b), 0) == iota((b, b), 1)
    bound_row = bound_ref[...]
    bound_col = jnp.sum(jnp.where(eye_b, bound_row, 0), axis=1, keepdims=True)
    here = iota((b, n), 1)
    count = jnp.sum(jnp.where(bound_col < here, 1, 0), axis=0, keepdims=True)
    is_bound = jnp.sum(jnp.where(bound_col == here, 1, 0), axis=0, keepdims=True)
    at = iota((1, n), 1)
    pos_row = jnp.where(is_bound > 0, count, b + at - count)
    here = iota((n, b), 0)
    count = jnp.sum(jnp.where(bound_row < here, 1, 0), axis=1, keepdims=True)
    is_bound = jnp.sum(jnp.where(bound_row == here, 1, 0), axis=1, keepdims=True)
    at = iota((n, 1), 0)
    pos_col = jnp.where(is_bound > 0, count, b + at - count)
    perm_mask = iota((n, n), 0) == pos_row
    perm = jnp.where(perm_mask, 1.0, 0.0).astype(BF16)
    perm_t = jnp.where(iota((n, n), 1) == pos_col, 1.0, 0.0).astype(BF16)

    for load in loads[1:4]:
        load.wait()
    for load in loads[5:]:
        load.start()
    eye = iota((n, n), 0) == iota((n, n), 1)
    sr = hop_ref[0] + sigma_ref[0, 0, 0]
    si = sigma_ref[1, 0, 0]
    dr = energy_value - onsite_ref[...] - jnp.sum(jnp.where(eye, sr, 0.0), axis=0, keepdims=True)
    di = BROADENING - jnp.sum(jnp.where(eye, si, 0.0), axis=0, keepdims=True)
    magnitude = dr * dr + di * di
    dr, di = dr / magnitude, -di / magnitude
    nr = jnp.where(eye, 0.0, -sr)
    ni = jnp.where(eye, 0.0, -si)
    krh, krl = split(nr * dr - ni * di)
    kih, kil = split(nr * di + ni * dr)
    moved = dot(perm, jnp.concatenate([krh, kih, krl, kil], axis=1)).astype(BF16)
    krh, kih, krl, kil = (dot(moved[:, i * n : (i + 1) * n], perm_t).astype(BF16) for i in range(4))
    rows = iota((8, n), 0)
    pieces = jnp.zeros((8, n), F32)
    for i, d in enumerate((dr, di)):
        for j in range(3):
            part = d.astype(BF16).astype(F32)
            pieces = jnp.where(rows == 3 * i + j, part, pieces)
            d = d - part
    pieces = dot(pieces.astype(BF16), perm_t).T
    dr_col = pieces[:, 0:1] + pieces[:, 1:2] + pieces[:, 2:3]
    di_col = pieces[:, 3:4] + pieces[:, 4:5] + pieces[:, 5:6]

    def ordered(re, im):
        return jnp.concatenate([re[:, :b], im[:, :b], re[:, b:], im[:, b:]], axis=1)

    def store_rhs(ref, at, p, turned, columns):
        ref[at, 0:b, columns] = p[:b]
        ref[at, b : 2 * b, columns] = turned[:b]
        ref[at, 2 * b : 2 * b + r, columns] = p[b:]
        ref[at, 2 * b + r :, columns] = turned[b:]

    whole = slice(0, 2 * n)
    first = slice(0, 2 * b)
    rest = slice(2 * b, 2 * n)
    for i, p in enumerate((ordered(krh, kih), ordered(krl, kil))):
        khl[i] = p
        store_rhs(rhs, i, p, rot(p, b), whole)

    p = dot3(khl[0], khl[1], rhs[0], rhs[1])
    yv[...] = p
    for i, part in enumerate(split(p)):
        k2l[i] = part
        store_rhs(rhs, i, part, rot(part, b), whole)

    def identity(start, rows):
        row = iota((rows, 2 * n), 0) + start
        column = iota((rows, 2 * n), 1)
        orbital = jnp.where(column < b, column, jnp.where((column >= 2 * b) & (column < 2 * b + r), column - b, -1))
        return jnp.where(row == orbital, 1.0, 0.0)

    def y_rows(start, rows):
        at = slice(start, start + rows)
        k3 = dot3(khl[0, at], khl[1, at], rhs[0], rhs[1])
        u = identity(start, rows) - khl[0, at].astype(F32) - khl[1, at].astype(F32) + yv[at] - k3
        y = dr_col[at] * u + di_col[at] * rot(u, b)
        yv[at] = y
        for i, part in enumerate(split(y)):
            yl[i, at] = part

    def k4_columns(columns, turn):
        p = dot3(k2l[0], k2l[1], rhs[0, :, columns], rhs[1, :, columns])
        for i, part in enumerate(split(p)):
            store_rhs(k4r, i, part, turn(part), columns)

    def k4_columns(columns, turn):
        p = dot3(k2l[0], k2l[1], rhs[0, :, columns], rhs[1, :, columns])
        for i, part in enumerate(split(p)):
            store_rhs(k4r, i, part, turn(part), columns)

    k4_columns(first, lambda part: rot(part, b))
    y_rows(0, b)
    corner = yv[:b, first] + dot3(yl[0, :b], yl[1, :b], k4r[0, :, first], k4r[1, :, first])
    loads[4].wait()
    c_row = cpl_ref[...]
    c_col = jnp.sum(jnp.where(eye_b, c_row, 0.0), axis=1, keepdims=True)
    c_both = c_col * c_row
    s_ref[0] = corner[:, :b] * c_both
    s_ref[1] = corner[:, b:] * c_both

    pl.semaphore_wait(barrier, 3 + ahead.astype(jnp.int32) + behind.astype(jnp.int32))
    step1 = remote(s_ref.at[1 - core], r1_ref, schur_send.at[0], schur_recv.at[0], {"slab": other_core})
    step1.start()
    @apart
    def _():
        k4_columns(rest, rot_rest)

    step1.wait()
    h2_ref[...] = s_ref[core] + r1_ref[...]
    step2 = remote(h2_ref, r2_ref, schur_send.at[1], schur_recv.at[1], {"slab": other_chip})
    step2.start()

    def finish_inverse():
        y_rows(b, r)
        a = yv[...] + dot3(yl[0], yl[1], k4r[0], k4r[1])
        av[...] = a
        for i, part in enumerate(split(a[:, first])):
            al[i] = part
        for i, part in enumerate(split(a[:b])):
            rr[i, :b] = part
            rr[i, b:] = rot(part, b)

    apart(finish_inverse)

    step2.wait()
    f_ref[core] = h2_ref[...] + r2_ref[...]
    step3 = remote(f_ref.at[core], f_ref.at[core], schur_send.at[2], schur_recv.at[2], {"slab": other_core})
    step3.start()
    loads[5].wait()
    loads[6].wait()

    def order_vertex():
        for i, part in enumerate(split(vertex_ref[0])):
            v = dot(part, perm_t)
            vp[i] = v.astype(BF16)
            vt[i] = v.T.astype(BF16)

    apart(order_vertex)
    step3.wait()

    tr = jnp.where(eye_b, 0.0, -ham_ref[...] - f_ref[0])
    ti = jnp.where(eye_b, 0.0, -f_ref[1])
    diag_r = jnp.where(eye_b, energy_value - ham_ref[...] - f_ref[0], 0.0)
    diag_i = jnp.where(eye_b, BROADENING - f_ref[1], 0.0)

    def reciprocal(axis):
        zr = jnp.sum(diag_r, axis=axis, keepdims=True)
        zi = jnp.sum(diag_i, axis=axis, keepdims=True)
        size = zr * zr + zi * zi
        return zr / size, -zi / size

    er, ei = reciprocal(0)
    er_col, ei_col = reciprocal(1)
    k = jnp.concatenate([tr * er - ti * ei, tr * ei + ti * er], axis=1)

    def turned(parts):
        return [jnp.concatenate([part, rot(part, b)], axis=0) for part in parts]

    one = jnp.where(iota((b, 2 * b), 0) == iota((b, 2 * b), 1), 1.0, 0.0)
    kl = split(k)
    k2 = dot3(*kl, *turned(kl))
    k2s = split(k2)
    k2t = turned(k2s)
    k3 = dot3(*kl, *k2t)
    k4 = dot3(*k2s, *k2t)
    u = one - k + k2 - k3
    u = er_col * u + ei_col * rot(u, b)
    t = u + dot3(*split(u), *turned(split(k4)))
    t = t * jnp.concatenate([c_both, c_both], axis=1)
    th, tl = turned(split(t))

    w = [[jnp.float32(0.0), jnp.float32(0.0)], [jnp.float32(0.0), jnp.float32(0.0)]]
    for way in range(2):
        for d in range(2):
            for m in range(2):
                w[way][d] = w[way][d] + jnp.where(steps_ref[m] == d + 1, weights_ref[way, m], 0.0)
    is_odd = odd == 1
    w_sum_own = jnp.where(is_odd, w[1][1], w[0][1])
    w_sum_pair = jnp.where(is_odd, w[1][0], w[0][0])
    w_pair = jnp.where(is_odd, w[0][0], w[1][0])
    w_one = jnp.where(is_odd, w[0][1], w[1][1])

    chunks = n // CHUNK
    def x_copy(at, c):
        return remote(g_ref.at[at], x_ref.at[at], x_send, x_recv.at[c], {"energy": pair})

    def one_copy(at, c):
        return remote(g_ref.at[at], one_ref.at[at], one_send, one_recv.at[c], {"energy": one_to})

    def sum_copy(at, c):
        return remote(sum_ref.at[at], got_ref.at[at], sum_send, sum_recv.at[c], {"energy": sum_to})

    def rows_of(c, size=CHUNK):
        return pl.ds(c * size, size)

    def send(c):
        x_copy(rows_of(c), c).start()
        end = (c + 1) * CHUNK
        if end % PART == 0:
            at = pl.ds(end - PART, PART)
            pl.when(ahead)(lambda: one_copy(at, (end - 1) // ONE).start())

    th_ref[0], th_ref[1] = th, tl

    def greens(start, rows):
        at = slice(start, start + rows)
        middle = dot3(al[0, at], al[1, at], th_ref[0], th_ref[1])
        g_ref[at] = av[at] + dot3(*split(middle), rr[0], rr[1])

    start = 0
    for rows in GROUPS:
        apart(functools.partial(greens, start, rows))
        for c in range(start // CHUNK, min((start + rows) // CHUNK, WINDOW)):
            send(c)
        start += rows

    def mix(start):
        at = slice(start, start + MIX)
        mixed = w_pair * x_ref[at]
        mixed = mixed + jnp.where(behind, w_one * one_ref[at], 0.0)
        mixed = mixed + jnp.where(ahead, got_ref[at], 0.0)
        stacked = jnp.concatenate(
            [
                jnp.concatenate([mixed[:, :b], mixed[:, 2 * b : 2 * b + r]], axis=1),
                jnp.concatenate([mixed[:, b : 2 * b], mixed[:, 2 * b + r :]], axis=1),
            ],
            axis=0,
        )
        dressed = dot3(*split(stacked), vt[0], vt[1])
        for i, part in enumerate(split(dressed)):
            q[i, at, :n] = part[:MIX]
            q[i, at, n:] = part[MIX:]
        if start + MIX == n - b:
            early = slice(0, n - b)
            acc[...] = dot3(vp[0, :, early], vp[1, :, early], q[0, early], q[1, early])

    for c in range(chunks + LAG):
        if c < chunks:
            x_copy(rows_of(c), c).wait_recv()
            at = slice(c * CHUNK, (c + 1) * CHUNK)
            sum_ref[at] = w_sum_own * g_ref[at] + w_sum_pair * x_ref[at]
            pl.when(behind)(lambda: sum_copy(rows_of(c), c).start())
            if c + WINDOW < chunks:
                send(c + WINDOW)
        if c >= LAG:
            done = c - LAG
            if done * CHUNK % ONE == 0:
                at = done * CHUNK // ONE
                pl.when(behind)(lambda: one_copy(rows_of(at, ONE), at).wait_recv())
            pl.when(ahead)(lambda: sum_copy(rows_of(done), done).wait_recv())
            if (done + 1) * CHUNK % MIX == 0:
                apart(functools.partial(mix, (done + 1) * CHUNK - MIX))
    late = slice(n - b, n)
    stores = []
    for i in range(2):
        half = slice(i * n, (i + 1) * n)
        res_ref[i] = acc[:, half] + dot3(vp[0, :, late], vp[1, :, late], q[0, late, half], q[1, late, half])
        store = pltpu.make_async_copy(res_ref.at[i], out_ref.at[i, 0, 0], out_sem.at[i])
        store.start()
        stores.append(store)
    every = pl.ds(0, n)
    x_copy(every, 0).wait_send()
    pl.when(ahead)(lambda: one_copy(every, 0).wait_send())
    pl.when(behind)(lambda: sum_copy(every, 0).wait_send())
    for store in stores:
        store.wait()


def per_device(*arrays):
    n = arrays[1].shape[-1]
    b = arrays[2].shape[0]
    chunks = n // CHUNK
    hbm = pl.BlockSpec(memory_space=pl.ANY)
    smem = pl.BlockSpec(memory_space=pltpu.SMEM)
    dma = pltpu.SemaphoreType.DMA
    return pl.pallas_call(
        kernel,
        out_shape=jax.ShapeDtypeStruct(arrays[5].shape, F32),
        in_specs=[hbm] * 7 + [smem] * 2,
        out_specs=hbm,
        scratch_shapes=[
            *(pltpu.VMEM(a.shape, a.dtype) for a in arrays[:7]),
            pltpu.VMEM((2, n, n), F32),
            dma((7,)),
            dma((2,)),
            pltpu.VMEM((2, n, 2 * n), BF16),
            pltpu.VMEM((2, 2 * n, 2 * n), BF16),
            pltpu.VMEM((2, n, 2 * n), BF16),
            pltpu.VMEM((2, 2 * n, 2 * n), BF16),
            pltpu.VMEM((n, 2 * n), F32),
            pltpu.VMEM((2, n, 2 * n), BF16),
            pltpu.VMEM((n, 2 * n), F32),
            pltpu.VMEM((2, n, 2 * b), BF16),
            pltpu.VMEM((2, 2 * b, 2 * n), BF16),
            pltpu.VMEM((2, n, n), BF16),
            pltpu.VMEM((2, n, n), BF16),
            pltpu.VMEM((2, n, 2 * n), BF16),
            pltpu.VMEM((n, 2 * n), F32),
            pltpu.VMEM((2, 2 * b, 2 * b), BF16),
            pltpu.VMEM((2, b, b), F32),
            pltpu.VMEM((b, b), F32),
            pltpu.VMEM((b, b), F32),
            pltpu.VMEM((b, b), F32),
            pltpu.VMEM((2, b, b), F32),
            pltpu.VMEM((n, 2 * n), F32),
            pltpu.VMEM((n, 2 * n), F32),
            pltpu.VMEM((n, 2 * n), F32),
            pltpu.VMEM((n, 2 * n), F32),
            pltpu.VMEM((n, 2 * n), F32),
            dma((3,)),
            dma((3,)),
            dma,
            dma((chunks,)),
            dma,
            dma((n // ONE,)),
            dma,
            dma((chunks,)),
        ],
        compiler_params=pltpu.CompilerParams(
            collective_id=0, has_side_effects=True, vmem_limit_bytes=60 * 2**20
        ),
    )(*arrays)


def solution(mesh):
    placed = (
        P("slab", None),
        P("slab", None, None),
        P(),
        P("slab", None),
        P("slab", None),
        P(None, "energy", "slab", None, None),
        P("slab", None, None),
        P(),
        P(),
    )
    return jax.shard_map(
        per_device,
        mesh=mesh,
        in_specs=placed,
        out_specs=P(None, "energy", "slab", None, None),
        check_vma=False,
    )
```

```python
import functools

import jax
import jax.numpy as jnp
from jax import lax
from jax.experimental import pallas as pl
from jax.experimental.pallas import tpu as pltpu
from jax.sharding import PartitionSpec as P

BROADENING = 1.0
LOWEST = -2.0
SPREAD = 4.0
CHUNK = 32
MIX = CHUNK
ONE = 64
WINDOW = 3
LAG = 2
FIRST = 64
F32 = jnp.float32
BF16 = jnp.bfloat16


def split(x):
    high = x.astype(BF16)
    return high, (x - high.astype(F32)).astype(BF16)


def dot(x, y):
    return jnp.dot(x, y, preferred_element_type=F32)


def dot3(xh, xl, yh, yl):
    return dot(jnp.concatenate([xh, xh, xl], axis=1), jnp.concatenate([yh, yl, yh], axis=0))


def rot(p, b):
    r = (p.shape[1] - 2 * b) // 2
    parts = [-p[:, b : 2 * b], p[:, :b]]
    if r:
        parts += [-p[:, 2 * b + r :], p[:, 2 * b : 2 * b + r]]
    return jnp.concatenate(parts, axis=1)


def rot_rest(p):
    r = p.shape[1] // 2
    return jnp.concatenate([-p[:, r:], p[:, :r]], axis=1)


def iota(shape, axis):
    return lax.broadcasted_iota(jnp.int32, shape, axis)


def kernel(
    onsite_in,
    hop_in,
    ham_in,
    cpl_in,
    bound_in,
    sigma_in,
    vertex_in,
    steps_ref,
    weights_ref,
    out_ref,
    onsite_ref,
    hop_ref,
    ham_ref,
    cpl_ref,
    bound_ref,
    sigma_ref,
    vertex_ref,
    res_ref,
    in_sem,
    out_sem,
    khl,
    rhs,
    k2l,
    k4r,
    yv,
    yl,
    av,
    al,
    rr,
    vp,
    vt,
    q,
    acc,
    th_ref,
    s_ref,
    r1_ref,
    h2_ref,
    r2_ref,
    f_ref,
    g_ref,
    x_ref,
    one_ref,
    sum_ref,
    got_ref,
    pair_ref,
    schur_send,
    schur_recv,
    x_send,
    x_recv,
    one_send,
    one_recv,
    sum_send,
    sum_recv,
):
    n = hop_ref.shape[-1]
    b = ham_ref.shape[0]
    r = n - b
    slab = lax.axis_index("slab")
    e = lax.axis_index("energy")
    energies = lax.axis_size("energy")
    core = lax.rem(slab, 2)
    other_core = slab + 1 - 2 * core
    other_chip = lax.rem(slab + 2, 4)
    odd = lax.rem(e, 2)
    pair = e + 1 - 2 * odd
    one_to = e - 2 + 4 * odd
    sum_to = e + 2 - 4 * odd
    ahead = (one_to >= 0) & (one_to < energies)
    behind = (sum_to >= 0) & (sum_to < energies)
    one_to = lax.rem(one_to + energies, energies)
    sum_to = lax.rem(sum_to + energies, energies)

    loads = [
        pltpu.make_async_copy(src, dst, in_sem.at[i])
        for i, (src, dst) in enumerate(
            (
                (bound_in, bound_ref),
                (sigma_in, sigma_ref),
                (hop_in, hop_ref),
                (onsite_in, onsite_ref),
                (cpl_in, cpl_ref),
                (ham_in, ham_ref),
                (vertex_in, vertex_ref),
            )
        )
    ]
    for load in loads[:5]:
        load.start()
    barrier = pltpu.get_barrier_semaphore()

    def greet(target):
        pl.semaphore_signal(barrier, inc=1, device_id=target, device_id_type=pl.DeviceIdType.MESH)

    greet({"slab": other_core})
    greet({"slab": other_chip})
    greet({"energy": pair})
    pl.when(ahead)(lambda: greet({"energy": one_to}))
    pl.when(behind)(lambda: greet({"energy": sum_to}))

    def remote(src, dst, send, recv, target):
        return pltpu.make_async_remote_copy(
            src_ref=src,
            dst_ref=dst,
            send_sem=send,
            recv_sem=recv,
            device_id=target,
            device_id_type=pl.DeviceIdType.MESH,
        )

    def apart(work):
        pl.when(slab >= 0)(work)

    energy_value = LOWEST + SPREAD * (e.astype(F32) + 0.5) / energies

    loads[0].wait()
    eye_b = iota((b, b), 0) == iota((b, b), 1)
    bound_row = bound_ref[...]
    bound_col = jnp.sum(jnp.where(eye_b, bound_row, 0), axis=1, keepdims=True)
    here = iota((b, n), 1)
    count = jnp.sum(jnp.where(bound_col < here, 1, 0), axis=0, keepdims=True)
    is_bound = jnp.sum(jnp.where(bound_col == here, 1, 0), axis=0, keepdims=True)
    at = iota((1, n), 1)
    pos_row = jnp.where(is_bound > 0, count, b + at - count)
    here = iota((n, b), 0)
    count = jnp.sum(jnp.where(bound_row < here, 1, 0), axis=1, keepdims=True)
    is_bound = jnp.sum(jnp.where(bound_row == here, 1, 0), axis=1, keepdims=True)
    at = iota((n, 1), 0)
    pos_col = jnp.where(is_bound > 0, count, b + at - count)
    perm_mask = iota((n, n), 0) == pos_row
    perm = jnp.where(perm_mask, 1.0, 0.0).astype(BF16)
    perm_t = jnp.where(iota((n, n), 1) == pos_col, 1.0, 0.0).astype(BF16)

    for load in loads[1:4]:
        load.wait()
    for load in loads[5:]:
        load.start()
    eye = iota((n, n), 0) == iota((n, n), 1)
    sr = hop_ref[0] + sigma_ref[0, 0, 0]
    si = sigma_ref[1, 0, 0]
    dr = energy_value - onsite_ref[...] - jnp.sum(jnp.where(eye, sr, 0.0), axis=0, keepdims=True)
    di = BROADENING - jnp.sum(jnp.where(eye, si, 0.0), axis=0, keepdims=True)
    magnitude = dr * dr + di * di
    dr, di = dr / magnitude, -di / magnitude
    nr = jnp.where(eye, 0.0, -sr)
    ni = jnp.where(eye, 0.0, -si)
    krh, krl = split(nr * dr - ni * di)
    kih, kil = split(nr * di + ni * dr)
    moved = dot(perm, jnp.concatenate([krh, kih, krl, kil], axis=1)).astype(BF16)
    krh, kih, krl, kil = (dot(moved[:, i * n : (i + 1) * n], perm_t).astype(BF16) for i in range(4))
    rows = iota((8, n), 0)
    pieces = jnp.zeros((8, n), F32)
    for i, d in enumerate((dr, di)):
        for j in range(3):
            part = d.astype(BF16).astype(F32)
            pieces = jnp.where(rows == 3 * i + j, part, pieces)
            d = d - part
    pieces = dot(pieces.astype(BF16), perm_t).T
    dr_col = pieces[:, 0:1] + pieces[:, 1:2] + pieces[:, 2:3]
    di_col = pieces[:, 3:4] + pieces[:, 4:5] + pieces[:, 5:6]

    def ordered(re, im):
        return jnp.concatenate([re[:, :b], im[:, :b], re[:, b:], im[:, b:]], axis=1)

    def store_rhs(ref, at, p, turned, columns):
        ref[at, 0:b, columns] = p[:b]
        ref[at, b : 2 * b, columns] = turned[:b]
        ref[at, 2 * b : 2 * b + r, columns] = p[b:]
        ref[at, 2 * b + r :, columns] = turned[b:]

    whole = slice(0, 2 * n)
    first = slice(0, 2 * b)
    rest = slice(2 * b, 2 * n)
    for i, p in enumerate((ordered(krh, kih), ordered(krl, kil))):
        khl[i] = p
        store_rhs(rhs, i, p, rot(p, b), whole)

    p = dot3(khl[0], khl[1], rhs[0], rhs[1])
    yv[...] = p
    for i, part in enumerate(split(p)):
        k2l[i] = part
        store_rhs(rhs, i, part, rot(part, b), whole)

    def identity(start, rows):
        row = iota((rows, 2 * n), 0) + start
        column = iota((rows, 2 * n), 1)
        orbital = jnp.where(column < b, column, jnp.where((column >= 2 * b) & (column < 2 * b + r), column - b, -1))
        return jnp.where(row == orbital, 1.0, 0.0)

    def y_rows(start, rows):
        at = slice(start, start + rows)
        k3 = dot3(khl[0, at], khl[1, at], rhs[0], rhs[1])
        u = identity(start, rows) - khl[0, at].astype(F32) - khl[1, at].astype(F32) + yv[at] - k3
        y = dr_col[at] * u + di_col[at] * rot(u, b)
        yv[at] = y
        for i, part in enumerate(split(y)):
            yl[i, at] = part

    def k4_columns(columns, turn):
        p = dot3(k2l[0], k2l[1], rhs[0, :, columns], rhs[1, :, columns])
        for i, part in enumerate(split(p)):
            store_rhs(k4r, i, part, turn(part), columns)

    def k4_columns(columns, turn):
        p = dot3(k2l[0], k2l[1], rhs[0, :, columns], rhs[1, :, columns])
        for i, part in enumerate(split(p)):
            store_rhs(k4r, i, part, turn(part), columns)

    k4_columns(first, lambda part: rot(part, b))
    y_rows(0, b)
    corner = yv[:b, first] + dot3(yl[0, :b], yl[1, :b], k4r[0, :, first], k4r[1, :, first])
    loads[4].wait()
    c_row = cpl_ref[...]
    c_col = jnp.sum(jnp.where(eye_b, c_row, 0.0), axis=1, keepdims=True)
    c_both = c_col * c_row
    s_ref[0] = corner[:, :b] * c_both
    s_ref[1] = corner[:, b:] * c_both

    pl.semaphore_wait(barrier, 3 + ahead.astype(jnp.int32) + behind.astype(jnp.int32))
    step1 = remote(s_ref.at[1 - core], r1_ref, schur_send.at[0], schur_recv.at[0], {"slab": other_core})
    step1.start()
    @apart
    def _():
        k4_columns(rest, rot_rest)

    step1.wait()
    h2_ref[...] = s_ref[core] + r1_ref[...]
    step2 = remote(h2_ref, r2_ref, schur_send.at[1], schur_recv.at[1], {"slab": other_chip})
    step2.start()

    def finish_inverse():
        y_rows(b, r)
        a = yv[...] + dot3(yl[0], yl[1], k4r[0], k4r[1])
        av[...] = a
        for i, part in enumerate(split(a[:, first])):
            al[i] = part
        for i, part in enumerate(split(a[:b])):
            rr[i, :b] = part
            rr[i, b:] = rot(part, b)

    apart(finish_inverse)

    step2.wait()
    f_ref[core] = h2_ref[...] + r2_ref[...]
    step3 = remote(f_ref.at[core], f_ref.at[core], schur_send.at[2], schur_recv.at[2], {"slab": other_core})
    step3.start()
    loads[5].wait()
    loads[6].wait()

    def order_vertex():
        for i, part in enumerate(split(vertex_ref[0])):
            v = dot(part, perm_t)
            vp[i] = v.astype(BF16)
            vt[i] = v.T.astype(BF16)

    apart(order_vertex)
    step3.wait()

    tr = jnp.where(eye_b, 0.0, -ham_ref[...] - f_ref[0])
    ti = jnp.where(eye_b, 0.0, -f_ref[1])
    diag_r = jnp.where(eye_b, energy_value - ham_ref[...] - f_ref[0], 0.0)
    diag_i = jnp.where(eye_b, BROADENING - f_ref[1], 0.0)

    def reciprocal(axis):
        zr = jnp.sum(diag_r, axis=axis, keepdims=True)
        zi = jnp.sum(diag_i, axis=axis, keepdims=True)
        size = zr * zr + zi * zi
        return zr / size, -zi / size

    er, ei = reciprocal(0)
    er_col, ei_col = reciprocal(1)
    k = jnp.concatenate([tr * er - ti * ei, tr * ei + ti * er], axis=1)

    def turned(parts):
        return [jnp.concatenate([part, rot(part, b)], axis=0) for part in parts]

    one = jnp.where(iota((b, 2 * b), 0) == iota((b, 2 * b), 1), 1.0, 0.0)
    kl = split(k)
    k2 = dot3(*kl, *turned(kl))
    k2s = split(k2)
    k2t = turned(k2s)
    k3 = dot3(*kl, *k2t)
    k4 = dot3(*k2s, *k2t)
    u = one - k + k2 - k3
    u = er_col * u + ei_col * rot(u, b)
    t = u + dot3(*split(u), *turned(split(k4)))
    t = t * jnp.concatenate([c_both, c_both], axis=1)
    th, tl = turned(split(t))

    w = [[jnp.float32(0.0), jnp.float32(0.0)], [jnp.float32(0.0), jnp.float32(0.0)]]
    for way in range(2):
        for d in range(2):
            for m in range(2):
                w[way][d] = w[way][d] + jnp.where(steps_ref[m] == d + 1, weights_ref[way, m], 0.0)
    is_odd = odd == 1
    w_sum_own = jnp.where(is_odd, w[1][1], w[0][1])
    w_sum_pair = jnp.where(is_odd, w[1][0], w[0][0])
    w_pair = jnp.where(is_odd, w[0][0], w[1][0])
    w_one = jnp.where(is_odd, w[0][1], w[1][1])

    chunks = n // CHUNK
    def x_copy(at, c):
        return remote(g_ref.at[at], x_ref.at[at], x_send, x_recv.at[c], {"energy": pair})

    def one_copy(at, c):
        return remote(g_ref.at[at], one_ref.at[at], one_send, one_recv.at[c], {"energy": one_to})

    def sum_copy(at, c):
        return remote(sum_ref.at[at], got_ref.at[at], sum_send, sum_recv.at[c], {"energy": sum_to})

    def rows_of(c, size=CHUNK):
        return pl.ds(c * size, size)

    def send_one(c):
        at = rows_of(c)
        pl.when(ahead)(lambda: one_copy(at, c * CHUNK // ONE).start())

    def send(c):
        x_copy(rows_of(c), c).start()
        send_one(c)

    th_ref[0], th_ref[1] = th, tl

    def greens(start, rows):
        at = slice(start, start + rows)
        middle = dot3(al[0, at], al[1, at], th_ref[0], th_ref[1])
        g_ref[at] = av[at] + dot3(*split(middle), rr[0], rr[1])

    flipped = list(range(FIRST // CHUNK))
    order = list(range(b // CHUNK, chunks)) + list(range(FIRST // CHUNK, b // CHUNK))
    apart(functools.partial(greens, b, CHUNK))
    send(order[0])
    apart(functools.partial(greens, 0, FIRST))
    for c in flipped:
        raw = remote(g_ref.at[rows_of(c)], got_ref.at[rows_of(c)], sum_send, sum_recv.at[c], {"energy": sum_to})
        pl.when(behind)(raw.start)
        send_one(c)
    apart(functools.partial(greens, b + CHUNK, r - CHUNK))
    for c in order[1:WINDOW]:
        send(c)
    apart(functools.partial(greens, FIRST, b - FIRST))

    def pair_copy(c):
        return remote(pair_ref.at[rows_of(c)], x_ref.at[rows_of(c)], x_send, x_recv.at[c], {"energy": pair})

    def mix(start):
        at = slice(start, start + MIX)
        raw = start < FIRST
        mixed = x_ref[at] if raw else w_pair * x_ref[at]
        mixed = mixed + jnp.where(behind, w_one * one_ref[at], 0.0)
        mixed = mixed + jnp.where(ahead, w_sum_own * got_ref[at] if raw else got_ref[at], 0.0)
        stacked = jnp.concatenate(
            [
                jnp.concatenate([mixed[:, :b], mixed[:, 2 * b : 2 * b + r]], axis=1),
                jnp.concatenate([mixed[:, b : 2 * b], mixed[:, 2 * b + r :]], axis=1),
            ],
            axis=0,
        )
        dressed = dot3(*split(stacked), vt[0], vt[1])
        for i, part in enumerate(split(dressed)):
            q[i, at, :n] = part[:MIX]
            q[i, at, n:] = part[MIX:]
        if start + MIX == n:
            early = slice(b, n)
            acc[...] = dot3(vp[0, :, early], vp[1, :, early], q[0, early], q[1, early])

    seen = set()
    for i in range(chunks + LAG):
        if i < len(order):
            c = order[i]
            x_copy(rows_of(c), c).wait_recv()
            at = slice(c * CHUNK, (c + 1) * CHUNK)
            sum_ref[at] = w_sum_own * g_ref[at] + w_sum_pair * x_ref[at]
            pl.when(behind)(lambda: sum_copy(rows_of(c), c).start())
            later = i + WINDOW
            if later < len(order):
                send(order[later])
            elif later < chunks:
                c = flipped[later - len(order)]
                group = c * CHUNK // ONE
                if group not in seen:
                    seen.add(group)
                    pl.when(behind)(lambda: one_copy(rows_of(group, ONE), group).wait_recv())
                at = slice(c * CHUNK, (c + 1) * CHUNK)
                pair_ref[at] = w_sum_pair * g_ref[at] + jnp.where(behind, w_pair * one_ref[at], 0.0)
                pair_copy(c).start()
        if i >= LAG:
            c = (order + flipped)[i - LAG]
            group = c * CHUNK // ONE
            if group not in seen:
                seen.add(group)
                pl.when(behind)(lambda: one_copy(rows_of(group, ONE), group).wait_recv())
            if c in flipped:
                pair_copy(c).wait_recv()
            pl.when(ahead)(lambda: sum_copy(rows_of(c), c).wait_recv())
            apart(functools.partial(mix, c * CHUNK))
    late = slice(0, b)
    stores = []
    for i in range(2):
        half = slice(i * n, (i + 1) * n)
        res_ref[i] = acc[:, half] + dot3(vp[0, :, late], vp[1, :, late], q[0, late, half], q[1, late, half])
        store = pltpu.make_async_copy(res_ref.at[i], out_ref.at[i, 0, 0], out_sem.at[i])
        store.start()
        stores.append(store)
    every = pl.ds(0, n)
    x_copy(every, 0).wait_send()
    pl.when(ahead)(lambda: one_copy(every, 0).wait_send())
    pl.when(behind)(lambda: sum_copy(every, 0).wait_send())
    for store in stores:
        store.wait()


def per_device(*arrays):
    n = arrays[1].shape[-1]
    b = arrays[2].shape[0]
    chunks = n // CHUNK
    hbm = pl.BlockSpec(memory_space=pl.ANY)
    smem = pl.BlockSpec(memory_space=pltpu.SMEM)
    dma = pltpu.SemaphoreType.DMA
    return pl.pallas_call(
        kernel,
        out_shape=jax.ShapeDtypeStruct(arrays[5].shape, F32),
        in_specs=[hbm] * 7 + [smem] * 2,
        out_specs=hbm,
        scratch_shapes=[
            *(pltpu.VMEM(a.shape, a.dtype) for a in arrays[:7]),
            pltpu.VMEM((2, n, n), F32),
            dma((7,)),
            dma((2,)),
            pltpu.VMEM((2, n, 2 * n), BF16),
            pltpu.VMEM((2, 2 * n, 2 * n), BF16),
            pltpu.VMEM((2, n, 2 * n), BF16),
            pltpu.VMEM((2, 2 * n, 2 * n), BF16),
            pltpu.VMEM((n, 2 * n), F32),
            pltpu.VMEM((2, n, 2 * n), BF16),
            pltpu.VMEM((n, 2 * n), F32),
            pltpu.VMEM((2, n, 2 * b), BF16),
            pltpu.VMEM((2, 2 * b, 2 * n), BF16),
            pltpu.VMEM((2, n, n), BF16),
            pltpu.VMEM((2, n, n), BF16),
            pltpu.VMEM((2, n, 2 * n), BF16),
            pltpu.VMEM((n, 2 * n), F32),
            pltpu.VMEM((2, 2 * b, 2 * b), BF16),
            pltpu.VMEM((2, b, b), F32),
            pltpu.VMEM((b, b), F32),
            pltpu.VMEM((b, b), F32),
            pltpu.VMEM((b, b), F32),
            pltpu.VMEM((2, b, b), F32),
            pltpu.VMEM((n, 2 * n), F32),
            pltpu.VMEM((n, 2 * n), F32),
            pltpu.VMEM((n, 2 * n), F32),
            pltpu.VMEM((n, 2 * n), F32),
            pltpu.VMEM((n, 2 * n), F32),
            pltpu.VMEM((FIRST, 2 * n), F32),
            dma((3,)),
            dma((3,)),
            dma,
            dma((chunks,)),
            dma,
            dma((n // ONE,)),
            dma,
            dma((chunks,)),
        ],
        compiler_params=pltpu.CompilerParams(
            collective_id=0, has_side_effects=True, vmem_limit_bytes=60 * 2**20
        ),
    )(*arrays)


def solution(mesh):
    placed = (
        P("slab", None),
        P("slab", None, None),
        P(),
        P("slab", None),
        P("slab", None),
        P(None, "energy", "slab", None, None),
        P("slab", None, None),
        P(),
        P(),
    )
    return jax.shard_map(
        per_device,
        mesh=mesh,
        in_specs=placed,
        out_specs=P(None, "energy", "slab", None, None),
        check_vma=False,
    )
```

```python
import functools

import jax
import jax.numpy as jnp
from jax import lax
from jax.experimental import pallas as pl
from jax.experimental.pallas import tpu as pltpu
from jax.sharding import PartitionSpec as P

BROADENING = 1.0
LOWEST = -2.0
SPREAD = 4.0
CHUNK = 32
MIX = CHUNK
ONE = 64
WINDOW = 3
LAG = 2
FIRST = 64
F32 = jnp.float32
BF16 = jnp.bfloat16


def split(x):
    high = x.astype(BF16)
    return high, (x - high.astype(F32)).astype(BF16)


def dot(x, y):
    return jnp.dot(x, y, preferred_element_type=F32)


def dot3(xh, xl, yh, yl):
    return dot(jnp.concatenate([xh, xh, xl], axis=1), jnp.concatenate([yh, yl, yh], axis=0))


def rot(p, b):
    r = (p.shape[1] - 2 * b) // 2
    parts = [-p[:, b : 2 * b], p[:, :b]]
    if r:
        parts += [-p[:, 2 * b + r :], p[:, 2 * b : 2 * b + r]]
    return jnp.concatenate(parts, axis=1)


def rot_rest(p):
    r = p.shape[1] // 2
    return jnp.concatenate([-p[:, r:], p[:, :r]], axis=1)


def iota(shape, axis):
    return lax.broadcasted_iota(jnp.int32, shape, axis)


def kernel(
    onsite_in,
    hop_in,
    ham_in,
    cpl_in,
    bound_in,
    sigma_in,
    vertex_in,
    steps_ref,
    weights_ref,
    out_ref,
    onsite_ref,
    hop_ref,
    ham_ref,
    cpl_ref,
    bound_ref,
    sigma_ref,
    vertex_ref,
    res_ref,
    in_sem,
    out_sem,
    khl,
    rhs,
    k2l,
    k4r,
    yv,
    yl,
    av,
    al,
    rr,
    vp,
    vt,
    q,
    acc,
    th_ref,
    s_ref,
    r1_ref,
    h2_ref,
    r2_ref,
    f_ref,
    g_ref,
    x_ref,
    one_ref,
    sum_ref,
    got_ref,
    pair_ref,
    schur_send,
    schur_recv,
    x_send,
    x_recv,
    one_send,
    one_recv,
    sum_send,
    sum_recv,
):
    n = hop_ref.shape[-1]
    b = ham_ref.shape[0]
    r = n - b
    slab = lax.axis_index("slab")
    e = lax.axis_index("energy")
    energies = lax.axis_size("energy")
    core = lax.rem(slab, 2)
    other_core = slab + 1 - 2 * core
    other_chip = lax.rem(slab + 2, 4)
    odd = lax.rem(e, 2)
    pair = e + 1 - 2 * odd
    one_to = e - 2 + 4 * odd
    sum_to = e + 2 - 4 * odd
    ahead = (one_to >= 0) & (one_to < energies)
    behind = (sum_to >= 0) & (sum_to < energies)
    one_to = lax.rem(one_to + energies, energies)
    sum_to = lax.rem(sum_to + energies, energies)

    loads = [
        pltpu.make_async_copy(src, dst, in_sem.at[i])
        for i, (src, dst) in enumerate(
            (
                (bound_in, bound_ref),
                (sigma_in, sigma_ref),
                (hop_in, hop_ref),
                (onsite_in, onsite_ref),
                (cpl_in, cpl_ref),
                (ham_in, ham_ref),
                (vertex_in, vertex_ref),
            )
        )
    ]
    for load in loads[:5]:
        load.start()
    barrier = pltpu.get_barrier_semaphore()

    def greet(target):
        pl.semaphore_signal(barrier, inc=1, device_id=target, device_id_type=pl.DeviceIdType.MESH)

    greet({"slab": other_core})
    greet({"slab": other_chip})
    greet({"energy": pair})
    pl.when(ahead)(lambda: greet({"energy": one_to}))
    pl.when(behind)(lambda: greet({"energy": sum_to}))

    def remote(src, dst, send, recv, target):
        return pltpu.make_async_remote_copy(
            src_ref=src,
            dst_ref=dst,
            send_sem=send,
            recv_sem=recv,
            device_id=target,
            device_id_type=pl.DeviceIdType.MESH,
        )

    def apart(work):
        pl.when(slab >= 0)(work)

    energy_value = LOWEST + SPREAD * (e.astype(F32) + 0.5) / energies

    loads[0].wait()
    eye_b = iota((b, b), 0) == iota((b, b), 1)
    bound_row = bound_ref[...]
    bound_col = jnp.sum(jnp.where(eye_b, bound_row, 0), axis=1, keepdims=True)
    here = iota((b, n), 1)
    count = jnp.sum(jnp.where(bound_col < here, 1, 0), axis=0, keepdims=True)
    is_bound = jnp.sum(jnp.where(bound_col == here, 1, 0), axis=0, keepdims=True)
    at = iota((1, n), 1)
    pos_row = jnp.where(is_bound > 0, count, b + at - count)
    here = iota((n, b), 0)
    count = jnp.sum(jnp.where(bound_row < here, 1, 0), axis=1, keepdims=True)
    is_bound = jnp.sum(jnp.where(bound_row == here, 1, 0), axis=1, keepdims=True)
    at = iota((n, 1), 0)
    pos_col = jnp.where(is_bound > 0, count, b + at - count)
    perm_mask = iota((n, n), 0) == pos_row
    perm = jnp.where(perm_mask, 1.0, 0.0).astype(BF16)
    perm_t = jnp.where(iota((n, n), 1) == pos_col, 1.0, 0.0).astype(BF16)

    for load in loads[1:4]:
        load.wait()
    for load in loads[5:]:
        load.start()
    eye = iota((n, n), 0) == iota((n, n), 1)
    sr = hop_ref[0] + sigma_ref[0, 0, 0]
    si = sigma_ref[1, 0, 0]
    dr = energy_value - onsite_ref[...] - jnp.sum(jnp.where(eye, sr, 0.0), axis=0, keepdims=True)
    di = BROADENING - jnp.sum(jnp.where(eye, si, 0.0), axis=0, keepdims=True)
    magnitude = dr * dr + di * di
    dr, di = dr / magnitude, -di / magnitude
    nr = jnp.where(eye, 0.0, -sr)
    ni = jnp.where(eye, 0.0, -si)
    krh, krl = split(nr * dr - ni * di)
    kih, kil = split(nr * di + ni * dr)
    moved = dot(perm, jnp.concatenate([krh, kih, krl, kil], axis=1)).astype(BF16)
    moved = jnp.concatenate([moved[:, i * n : (i + 1) * n] for i in range(4)], axis=0)
    moved = dot(moved, perm_t).astype(BF16)
    krh, kih, krl, kil = (moved[i * n : (i + 1) * n] for i in range(4))
    rows = iota((8, n), 0)
    pieces = jnp.zeros((8, n), F32)
    for i, d in enumerate((dr, di)):
        for j in range(3):
            part = d.astype(BF16).astype(F32)
            pieces = jnp.where(rows == 3 * i + j, part, pieces)
            d = d - part
    pieces = dot(pieces.astype(BF16), perm_t).T
    dr_col = pieces[:, 0:1] + pieces[:, 1:2] + pieces[:, 2:3]
    di_col = pieces[:, 3:4] + pieces[:, 4:5] + pieces[:, 5:6]

    def ordered(re, im):
        return jnp.concatenate([re[:, :b], im[:, :b], re[:, b:], im[:, b:]], axis=1)

    def store_rhs(ref, at, p, turned, columns):
        ref[at, 0:b, columns] = p[:b]
        ref[at, b : 2 * b, columns] = turned[:b]
        ref[at, 2 * b : 2 * b + r, columns] = p[b:]
        ref[at, 2 * b + r :, columns] = turned[b:]

    whole = slice(0, 2 * n)
    first = slice(0, 2 * b)
    rest = slice(2 * b, 2 * n)
    for i, p in enumerate((ordered(krh, kih), ordered(krl, kil))):
        khl[i] = p
        store_rhs(rhs, i, p, rot(p, b), whole)

    p = dot3(khl[0], khl[1], rhs[0], rhs[1])
    yv[...] = p
    for i, part in enumerate(split(p)):
        k2l[i] = part
        store_rhs(rhs, i, part, rot(part, b), whole)

    def identity(start, rows):
        row = iota((rows, 2 * n), 0) + start
        column = iota((rows, 2 * n), 1)
        orbital = jnp.where(column < b, column, jnp.where((column >= 2 * b) & (column < 2 * b + r), column - b, -1))
        return jnp.where(row == orbital, 1.0, 0.0)

    def y_rows(start, rows, k3=None):
        at = slice(start, start + rows)
        if k3 is None:
            k3 = dot3(khl[0, at], khl[1, at], rhs[0], rhs[1])
        u = identity(start, rows) - khl[0, at].astype(F32) - khl[1, at].astype(F32) + yv[at] - k3
        y = dr_col[at] * u + di_col[at] * rot(u, b)
        yv[at] = y
        for i, part in enumerate(split(y)):
            yl[i, at] = part

    def k4_columns(columns, turn):
        p = dot3(k2l[0], k2l[1], rhs[0, :, columns], rhs[1, :, columns])
        for i, part in enumerate(split(p)):
            store_rhs(k4r, i, part, turn(part), columns)

    stacked = [jnp.concatenate([khl[i, :b], k2l[i]], axis=0) for i in range(2)]
    stacked = dot3(*stacked, rhs[0, :, first], rhs[1, :, first])
    for i, part in enumerate(split(stacked[b:])):
        store_rhs(k4r, i, part, rot(part, b), first)
    k3 = dot3(khl[0, :b], khl[1, :b], rhs[0, :, rest], rhs[1, :, rest])
    y_rows(0, b, jnp.concatenate([stacked[:b], k3], axis=1))
    corner = yv[:b, first] + dot3(yl[0, :b], yl[1, :b], k4r[0, :, first], k4r[1, :, first])
    loads[4].wait()
    c_row = cpl_ref[...]
    c_col = jnp.sum(jnp.where(eye_b, c_row, 0.0), axis=1, keepdims=True)
    c_both = c_col * c_row
    s_ref[0] = corner[:, :b] * c_both
    s_ref[1] = corner[:, b:] * c_both

    pl.semaphore_wait(barrier, 3 + ahead.astype(jnp.int32) + behind.astype(jnp.int32))
    step1 = remote(s_ref.at[1 - core], r1_ref, schur_send.at[0], schur_recv.at[0], {"slab": other_core})
    step1.start()
    @apart
    def _():
        k4_columns(rest, rot_rest)

    step1.wait()
    h2_ref[...] = s_ref[core] + r1_ref[...]
    step2 = remote(h2_ref, r2_ref, schur_send.at[1], schur_recv.at[1], {"slab": other_chip})
    step2.start()

    def finish_inverse():
        y_rows(b, r)
        a = yv[...] + dot3(yl[0], yl[1], k4r[0], k4r[1])
        av[...] = a
        for i, part in enumerate(split(a[:, first])):
            al[i] = part
        for i, part in enumerate(split(a[:b])):
            rr[i, :b] = part
            rr[i, b:] = rot(part, b)

    apart(finish_inverse)

    step2.wait()
    f_ref[core] = h2_ref[...] + r2_ref[...]
    step3 = remote(f_ref.at[core], f_ref.at[core], schur_send.at[2], schur_recv.at[2], {"slab": other_core})
    step3.start()
    loads[5].wait()
    loads[6].wait()

    def order_vertex():
        for i, part in enumerate(split(vertex_ref[0])):
            v = dot(part, perm_t)
            vp[i] = v.astype(BF16)
            vt[i] = v.T.astype(BF16)

    apart(order_vertex)
    step3.wait()

    tr = jnp.where(eye_b, 0.0, -ham_ref[...] - f_ref[0])
    ti = jnp.where(eye_b, 0.0, -f_ref[1])
    diag_r = jnp.where(eye_b, energy_value - ham_ref[...] - f_ref[0], 0.0)
    diag_i = jnp.where(eye_b, BROADENING - f_ref[1], 0.0)

    def reciprocal(axis):
        zr = jnp.sum(diag_r, axis=axis, keepdims=True)
        zi = jnp.sum(diag_i, axis=axis, keepdims=True)
        size = zr * zr + zi * zi
        return zr / size, -zi / size

    er, ei = reciprocal(0)
    er_col, ei_col = reciprocal(1)
    k = jnp.concatenate([tr * er - ti * ei, tr * ei + ti * er], axis=1)

    def turned(parts):
        return [jnp.concatenate([part, rot(part, b)], axis=0) for part in parts]

    one = jnp.where(iota((b, 2 * b), 0) == iota((b, 2 * b), 1), 1.0, 0.0)
    kl = split(k)
    k2 = dot3(*kl, *turned(kl))
    k2s = split(k2)
    k2t = turned(k2s)
    both = dot3(*(jnp.concatenate(pieces, axis=0) for pieces in zip(kl, k2s)), *k2t)
    k3, k4 = both[:b], both[b:]
    u = one - k + k2 - k3
    u = er_col * u + ei_col * rot(u, b)
    t = u + dot3(*split(u), *turned(split(k4)))
    t = t * jnp.concatenate([c_both, c_both], axis=1)
    th, tl = turned(split(t))

    w = [[jnp.float32(0.0), jnp.float32(0.0)], [jnp.float32(0.0), jnp.float32(0.0)]]
    for way in range(2):
        for d in range(2):
            for m in range(2):
                w[way][d] = w[way][d] + jnp.where(steps_ref[m] == d + 1, weights_ref[way, m], 0.0)
    is_odd = odd == 1
    w_sum_own = jnp.where(is_odd, w[1][1], w[0][1])
    w_sum_pair = jnp.where(is_odd, w[1][0], w[0][0])
    w_pair = jnp.where(is_odd, w[0][0], w[1][0])
    w_one = jnp.where(is_odd, w[0][1], w[1][1])

    chunks = n // CHUNK
    def x_copy(at, c):
        return remote(g_ref.at[at], x_ref.at[at], x_send, x_recv.at[c], {"energy": pair})

    def one_copy(at, c):
        return remote(g_ref.at[at], one_ref.at[at], one_send, one_recv.at[c], {"energy": one_to})

    def sum_copy(at, c):
        return remote(sum_ref.at[at], got_ref.at[at], sum_send, sum_recv.at[c], {"energy": sum_to})

    def rows_of(c, size=CHUNK):
        return pl.ds(c * size, size)

    def send_one(c):
        at = rows_of(c)
        pl.when(ahead)(lambda: one_copy(at, c * CHUNK // ONE).start())

    def send(c):
        x_copy(rows_of(c), c).start()
        send_one(c)

    th_ref[0], th_ref[1] = th, tl

    def greens(start, rows):
        at = slice(start, start + rows)
        middle = dot3(al[0, at], al[1, at], th_ref[0], th_ref[1])
        g_ref[at] = av[at] + dot3(*split(middle), rr[0], rr[1])

    flipped = list(range(FIRST // CHUNK))
    order = list(range(b // CHUNK, chunks)) + list(range(FIRST // CHUNK, b // CHUNK))
    apart(functools.partial(greens, b, CHUNK))
    send(order[0])
    apart(functools.partial(greens, 0, FIRST))
    for c in flipped:
        raw = remote(g_ref.at[rows_of(c)], got_ref.at[rows_of(c)], sum_send, sum_recv.at[c], {"energy": sum_to})
        pl.when(behind)(raw.start)
        send_one(c)
    apart(functools.partial(greens, b + CHUNK, r - CHUNK))
    for c in order[1:WINDOW]:
        send(c)
    apart(functools.partial(greens, FIRST, b - FIRST))

    def pair_copy(c):
        return remote(pair_ref.at[rows_of(c)], x_ref.at[rows_of(c)], x_send, x_recv.at[c], {"energy": pair})

    def mix(start):
        at = slice(start, start + MIX)
        raw = start < FIRST
        mixed = x_ref[at] if raw else w_pair * x_ref[at]
        mixed = mixed + jnp.where(behind, w_one * one_ref[at], 0.0)
        mixed = mixed + jnp.where(ahead, w_sum_own * got_ref[at] if raw else got_ref[at], 0.0)
        stacked = jnp.concatenate(
            [
                jnp.concatenate([mixed[:, :b], mixed[:, 2 * b : 2 * b + r]], axis=1),
                jnp.concatenate([mixed[:, b : 2 * b], mixed[:, 2 * b + r :]], axis=1),
            ],
            axis=0,
        )
        dressed = dot3(*split(stacked), vt[0], vt[1])
        for i, part in enumerate(split(dressed)):
            q[i, at, :n] = part[:MIX]
            q[i, at, n:] = part[MIX:]
        if start + MIX == n:
            early = slice(b, n)
            acc[...] = dot3(vp[0, :, early], vp[1, :, early], q[0, early], q[1, early])

    seen = set()
    for i in range(chunks + LAG):
        if i < len(order):
            c = order[i]
            x_copy(rows_of(c), c).wait_recv()
            at = slice(c * CHUNK, (c + 1) * CHUNK)
            sum_ref[at] = w_sum_own * g_ref[at] + w_sum_pair * x_ref[at]
            pl.when(behind)(lambda: sum_copy(rows_of(c), c).start())
            later = i + WINDOW
            if later < len(order):
                send(order[later])
            elif later < chunks:
                c = flipped[later - len(order)]
                group = c * CHUNK // ONE
                if group not in seen:
                    seen.add(group)
                    pl.when(behind)(lambda: one_copy(rows_of(group, ONE), group).wait_recv())
                at = slice(c * CHUNK, (c + 1) * CHUNK)
                pair_ref[at] = w_sum_pair * g_ref[at] + jnp.where(behind, w_pair * one_ref[at], 0.0)
                pair_copy(c).start()
        if i >= LAG:
            c = (order + flipped)[i - LAG]
            group = c * CHUNK // ONE
            if group not in seen:
                seen.add(group)
                pl.when(behind)(lambda: one_copy(rows_of(group, ONE), group).wait_recv())
            if c in flipped:
                pair_copy(c).wait_recv()
            pl.when(ahead)(lambda: sum_copy(rows_of(c), c).wait_recv())
            apart(functools.partial(mix, c * CHUNK))
    late = slice(0, b)
    stores = []
    for i in range(2):
        half = slice(i * n, (i + 1) * n)
        res_ref[i] = acc[:, half] + dot3(vp[0, :, late], vp[1, :, late], q[0, late, half], q[1, late, half])
        store = pltpu.make_async_copy(res_ref.at[i], out_ref.at[i, 0, 0], out_sem.at[i])
        store.start()
        stores.append(store)
    every = pl.ds(0, n)
    x_copy(every, 0).wait_send()
    pl.when(ahead)(lambda: one_copy(every, 0).wait_send())
    pl.when(behind)(lambda: sum_copy(every, 0).wait_send())
    for store in stores:
        store.wait()


def per_device(*arrays):
    n = arrays[1].shape[-1]
    b = arrays[2].shape[0]
    chunks = n // CHUNK
    hbm = pl.BlockSpec(memory_space=pl.ANY)
    smem = pl.BlockSpec(memory_space=pltpu.SMEM)
    dma = pltpu.SemaphoreType.DMA
    return pl.pallas_call(
        kernel,
        out_shape=jax.ShapeDtypeStruct(arrays[5].shape, F32),
        in_specs=[hbm] * 7 + [smem] * 2,
        out_specs=hbm,
        scratch_shapes=[
            *(pltpu.VMEM(a.shape, a.dtype) for a in arrays[:7]),
            pltpu.VMEM((2, n, n), F32),
            dma((7,)),
            dma((2,)),
            pltpu.VMEM((2, n, 2 * n), BF16),
            pltpu.VMEM((2, 2 * n, 2 * n), BF16),
            pltpu.VMEM((2, n, 2 * n), BF16),
            pltpu.VMEM((2, 2 * n, 2 * n), BF16),
            pltpu.VMEM((n, 2 * n), F32),
            pltpu.VMEM((2, n, 2 * n), BF16),
            pltpu.VMEM((n, 2 * n), F32),
            pltpu.VMEM((2, n, 2 * b), BF16),
            pltpu.VMEM((2, 2 * b, 2 * n), BF16),
            pltpu.VMEM((2, n, n), BF16),
            pltpu.VMEM((2, n, n), BF16),
            pltpu.VMEM((2, n, 2 * n), BF16),
            pltpu.VMEM((n, 2 * n), F32),
            pltpu.VMEM((2, 2 * b, 2 * b), BF16),
            pltpu.VMEM((2, b, b), F32),
            pltpu.VMEM((b, b), F32),
            pltpu.VMEM((b, b), F32),
            pltpu.VMEM((b, b), F32),
            pltpu.VMEM((2, b, b), F32),
            pltpu.VMEM((n, 2 * n), F32),
            pltpu.VMEM((n, 2 * n), F32),
            pltpu.VMEM((n, 2 * n), F32),
            pltpu.VMEM((n, 2 * n), F32),
            pltpu.VMEM((n, 2 * n), F32),
            pltpu.VMEM((FIRST, 2 * n), F32),
            dma((3,)),
            dma((3,)),
            dma,
            dma((chunks,)),
            dma,
            dma((n // ONE,)),
            dma,
            dma((chunks,)),
        ],
        compiler_params=pltpu.CompilerParams(
            collective_id=0, has_side_effects=True, vmem_limit_bytes=60 * 2**20
        ),
    )(*arrays)


def solution(mesh):
    placed = (
        P("slab", None),
        P("slab", None, None),
        P(),
        P("slab", None),
        P("slab", None),
        P(None, "energy", "slab", None, None),
        P("slab", None, None),
        P(),
        P(),
    )
    return jax.shard_map(
        per_device,
        mesh=mesh,
        in_specs=placed,
        out_specs=P(None, "energy", "slab", None, None),
        check_vma=False,
    )
```

```python
import functools

import jax
import jax.numpy as jnp
from jax import lax
from jax.experimental import pallas as pl
from jax.experimental.pallas import tpu as pltpu
from jax.sharding import PartitionSpec as P

BROADENING = 1.0
LOWEST = -2.0
SPREAD = 4.0
CHUNK = 32
MIX = CHUNK
ONE = 64
WINDOW = 4
LAG = 2
FIRST = 64
F32 = jnp.float32
BF16 = jnp.bfloat16


def split(x):
    high = x.astype(BF16)
    return high, (x - high.astype(F32)).astype(BF16)


def dot(x, y):
    return jnp.dot(x, y, preferred_element_type=F32)


def dot3(xh, xl, yh, yl):
    return dot(jnp.concatenate([xh, xh, xl], axis=1), jnp.concatenate([yh, yl, yh], axis=0))


def rot(p, b):
    r = (p.shape[1] - 2 * b) // 2
    parts = [-p[:, b : 2 * b], p[:, :b]]
    if r:
        parts += [-p[:, 2 * b + r :], p[:, 2 * b : 2 * b + r]]
    return jnp.concatenate(parts, axis=1)


def rot_rest(p):
    r = p.shape[1] // 2
    return jnp.concatenate([-p[:, r:], p[:, :r]], axis=1)


def iota(shape, axis):
    return lax.broadcasted_iota(jnp.int32, shape, axis)


def kernel(
    onsite_in,
    hop_in,
    ham_in,
    cpl_in,
    bound_in,
    sigma_in,
    vertex_in,
    steps_ref,
    weights_ref,
    out_ref,
    onsite_ref,
    hop_ref,
    ham_ref,
    cpl_ref,
    bound_ref,
    sigma_ref,
    vertex_ref,
    res_ref,
    in_sem,
    out_sem,
    khl,
    rhs,
    k2l,
    k4r,
    yv,
    yl,
    av,
    al,
    rr,
    vp,
    vt,
    q,
    acc,
    th_ref,
    s_ref,
    r1_ref,
    h2_ref,
    r2_ref,
    f_ref,
    g_ref,
    x_ref,
    one_ref,
    sum_ref,
    got_ref,
    pair_ref,
    schur_send,
    schur_recv,
    x_send,
    x_recv,
    one_send,
    one_recv,
    sum_send,
    sum_recv,
):
    n = hop_ref.shape[-1]
    b = ham_ref.shape[0]
    r = n - b
    slab = lax.axis_index("slab")
    e = lax.axis_index("energy")
    energies = lax.axis_size("energy")
    core = lax.rem(slab, 2)
    other_core = slab + 1 - 2 * core
    other_chip = lax.rem(slab + 2, 4)
    odd = lax.rem(e, 2)
    pair = e + 1 - 2 * odd
    one_to = e - 2 + 4 * odd
    sum_to = e + 2 - 4 * odd
    ahead = (one_to >= 0) & (one_to < energies)
    behind = (sum_to >= 0) & (sum_to < energies)
    one_to = lax.rem(one_to + energies, energies)
    sum_to = lax.rem(sum_to + energies, energies)

    loads = [
        pltpu.make_async_copy(src, dst, in_sem.at[i])
        for i, (src, dst) in enumerate(
            (
                (bound_in, bound_ref),
                (sigma_in, sigma_ref),
                (hop_in, hop_ref),
                (onsite_in, onsite_ref),
                (cpl_in, cpl_ref),
                (ham_in, ham_ref),
                (vertex_in, vertex_ref),
            )
        )
    ]
    for load in loads[:5]:
        load.start()
    barrier = pltpu.get_barrier_semaphore()

    def greet(target):
        pl.semaphore_signal(barrier, inc=1, device_id=target, device_id_type=pl.DeviceIdType.MESH)

    greet({"slab": other_core})
    greet({"slab": other_chip})
    greet({"energy": pair})
    pl.when(ahead)(lambda: greet({"energy": one_to}))
    pl.when(behind)(lambda: greet({"energy": sum_to}))

    def remote(src, dst, send, recv, target):
        return pltpu.make_async_remote_copy(
            src_ref=src,
            dst_ref=dst,
            send_sem=send,
            recv_sem=recv,
            device_id=target,
            device_id_type=pl.DeviceIdType.MESH,
        )

    def apart(work):
        pl.when(slab >= 0)(work)

    energy_value = LOWEST + SPREAD * (e.astype(F32) + 0.5) / energies

    loads[0].wait()
    eye_b = iota((b, b), 0) == iota((b, b), 1)
    bound_row = bound_ref[...]
    bound_col = jnp.sum(jnp.where(eye_b, bound_row, 0), axis=1, keepdims=True)
    here = iota((b, n), 1)
    count = jnp.sum(jnp.where(bound_col < here, 1, 0), axis=0, keepdims=True)
    is_bound = jnp.sum(jnp.where(bound_col == here, 1, 0), axis=0, keepdims=True)
    at = iota((1, n), 1)
    pos_row = jnp.where(is_bound > 0, count, b + at - count)
    here = iota((n, b), 0)
    count = jnp.sum(jnp.where(bound_row < here, 1, 0), axis=1, keepdims=True)
    is_bound = jnp.sum(jnp.where(bound_row == here, 1, 0), axis=1, keepdims=True)
    at = iota((n, 1), 0)
    pos_col = jnp.where(is_bound > 0, count, b + at - count)
    perm_mask = iota((n, n), 0) == pos_row
    perm = jnp.where(perm_mask, 1.0, 0.0).astype(BF16)
    perm_t = jnp.where(iota((n, n), 1) == pos_col, 1.0, 0.0).astype(BF16)

    for load in loads[1:4]:
        load.wait()
    for load in loads[5:]:
        load.start()
    eye = iota((n, n), 0) == iota((n, n), 1)
    sr = hop_ref[0] + sigma_ref[0, 0, 0]
    si = sigma_ref[1, 0, 0]
    dr = energy_value - onsite_ref[...] - jnp.sum(jnp.where(eye, sr, 0.0), axis=0, keepdims=True)
    di = BROADENING - jnp.sum(jnp.where(eye, si, 0.0), axis=0, keepdims=True)
    magnitude = dr * dr + di * di
    dr, di = dr / magnitude, -di / magnitude
    nr = jnp.where(eye, 0.0, -sr)
    ni = jnp.where(eye, 0.0, -si)
    krh, krl = split(nr * dr - ni * di)
    kih, kil = split(nr * di + ni * dr)
    moved = dot(perm, jnp.concatenate([krh, kih, krl, kil], axis=1)).astype(BF16)
    moved = jnp.concatenate([moved[:, i * n : (i + 1) * n] for i in range(4)], axis=0)
    moved = dot(moved, perm_t).astype(BF16)
    krh, kih, krl, kil = (moved[i * n : (i + 1) * n] for i in range(4))
    rows = iota((8, n), 0)
    pieces = jnp.zeros((8, n), F32)
    for i, d in enumerate((dr, di)):
        for j in range(3):
            part = d.astype(BF16).astype(F32)
            pieces = jnp.where(rows == 3 * i + j, part, pieces)
            d = d - part
    pieces = dot(pieces.astype(BF16), perm_t).T
    dr_col = pieces[:, 0:1] + pieces[:, 1:2] + pieces[:, 2:3]
    di_col = pieces[:, 3:4] + pieces[:, 4:5] + pieces[:, 5:6]

    def ordered(re, im):
        return jnp.concatenate([re[:, :b], im[:, :b], re[:, b:], im[:, b:]], axis=1)

    def store_rhs(ref, at, p, turned, columns):
        ref[at, 0:b, columns] = p[:b]
        ref[at, b : 2 * b, columns] = turned[:b]
        ref[at, 2 * b : 2 * b + r, columns] = p[b:]
        ref[at, 2 * b + r :, columns] = turned[b:]

    whole = slice(0, 2 * n)
    first = slice(0, 2 * b)
    rest = slice(2 * b, 2 * n)
    for i, p in enumerate((ordered(krh, kih), ordered(krl, kil))):
        khl[i] = p
        store_rhs(rhs, i, p, rot(p, b), whole)

    p = dot3(khl[0], khl[1], rhs[0], rhs[1])
    yv[...] = p
    for i, part in enumerate(split(p)):
        k2l[i] = part
        store_rhs(rhs, i, part, rot(part, b), whole)

    def identity(start, rows):
        row = iota((rows, 2 * n), 0) + start
        column = iota((rows, 2 * n), 1)
        orbital = jnp.where(column < b, column, jnp.where((column >= 2 * b) & (column < 2 * b + r), column - b, -1))
        return jnp.where(row == orbital, 1.0, 0.0)

    def y_rows(start, rows, k3=None):
        at = slice(start, start + rows)
        if k3 is None:
            k3 = dot3(khl[0, at], khl[1, at], rhs[0], rhs[1])
        u = identity(start, rows) - khl[0, at].astype(F32) - khl[1, at].astype(F32) + yv[at] - k3
        y = dr_col[at] * u + di_col[at] * rot(u, b)
        yv[at] = y
        for i, part in enumerate(split(y)):
            yl[i, at] = part

    def k4_columns(columns, turn):
        p = dot3(k2l[0], k2l[1], rhs[0, :, columns], rhs[1, :, columns])
        for i, part in enumerate(split(p)):
            store_rhs(k4r, i, part, turn(part), columns)

    stacked = [jnp.concatenate([khl[i, :b], k2l[i]], axis=0) for i in range(2)]
    stacked = dot3(*stacked, rhs[0, :, first], rhs[1, :, first])
    for i, part in enumerate(split(stacked[b:])):
        store_rhs(k4r, i, part, rot(part, b), first)
    k3 = dot3(khl[0, :b], khl[1, :b], rhs[0, :, rest], rhs[1, :, rest])
    y_rows(0, b, jnp.concatenate([stacked[:b], k3], axis=1))
    corner = yv[:b, first] + dot3(yl[0, :b], yl[1, :b], k4r[0, :, first], k4r[1, :, first])
    loads[4].wait()
    c_row = cpl_ref[...]
    c_col = jnp.sum(jnp.where(eye_b, c_row, 0.0), axis=1, keepdims=True)
    c_both = c_col * c_row
    s_ref[0] = corner[:, :b] * c_both
    s_ref[1] = corner[:, b:] * c_both

    pl.semaphore_wait(barrier, 3 + ahead.astype(jnp.int32) + behind.astype(jnp.int32))
    step1 = remote(s_ref.at[1 - core], r1_ref, schur_send.at[0], schur_recv.at[0], {"slab": other_core})
    step1.start()
    @apart
    def _():
        k4_columns(rest, rot_rest)

    step1.wait()
    h2_ref[...] = s_ref[core] + r1_ref[...]
    step2 = remote(h2_ref, r2_ref, schur_send.at[1], schur_recv.at[1], {"slab": other_chip})
    step2.start()

    def finish_inverse():
        y_rows(b, r)
        a = yv[...] + dot3(yl[0], yl[1], k4r[0], k4r[1])
        av[...] = a
        for i, part in enumerate(split(a[:, first])):
            al[i] = part
        for i, part in enumerate(split(a[:b])):
            rr[i, :b] = part
            rr[i, b:] = rot(part, b)

    apart(finish_inverse)

    step2.wait()
    f_ref[core] = h2_ref[...] + r2_ref[...]
    step3 = remote(f_ref.at[core], f_ref.at[core], schur_send.at[2], schur_recv.at[2], {"slab": other_core})
    step3.start()
    loads[5].wait()
    loads[6].wait()

    def order_vertex():
        for i, part in enumerate(split(vertex_ref[0])):
            v = dot(part, perm_t)
            vp[i] = v.astype(BF16)
            vt[i] = v.T.astype(BF16)

    apart(order_vertex)
    step3.wait()

    tr = jnp.where(eye_b, 0.0, -ham_ref[...] - f_ref[0])
    ti = jnp.where(eye_b, 0.0, -f_ref[1])
    diag_r = jnp.where(eye_b, energy_value - ham_ref[...] - f_ref[0], 0.0)
    diag_i = jnp.where(eye_b, BROADENING - f_ref[1], 0.0)

    def reciprocal(axis):
        zr = jnp.sum(diag_r, axis=axis, keepdims=True)
        zi = jnp.sum(diag_i, axis=axis, keepdims=True)
        size = zr * zr + zi * zi
        return zr / size, -zi / size

    er, ei = reciprocal(0)
    er_col, ei_col = reciprocal(1)
    k = jnp.concatenate([tr * er - ti * ei, tr * ei + ti * er], axis=1)

    def turned(parts):
        return [jnp.concatenate([part, rot(part, b)], axis=0) for part in parts]

    one = jnp.where(iota((b, 2 * b), 0) == iota((b, 2 * b), 1), 1.0, 0.0)
    kl = split(k)
    k2 = dot3(*kl, *turned(kl))
    k2s = split(k2)
    k2t = turned(k2s)
    both = dot3(*(jnp.concatenate(pieces, axis=0) for pieces in zip(kl, k2s)), *k2t)
    k3, k4 = both[:b], both[b:]
    u = one - k + k2 - k3
    u = er_col * u + ei_col * rot(u, b)
    t = u + dot3(*split(u), *turned(split(k4)))
    t = t * jnp.concatenate([c_both, c_both], axis=1)
    th, tl = turned(split(t))

    w = [[jnp.float32(0.0), jnp.float32(0.0)], [jnp.float32(0.0), jnp.float32(0.0)]]
    for way in range(2):
        for d in range(2):
            for m in range(2):
                w[way][d] = w[way][d] + jnp.where(steps_ref[m] == d + 1, weights_ref[way, m], 0.0)
    is_odd = odd == 1
    w_sum_own = jnp.where(is_odd, w[1][1], w[0][1])
    w_sum_pair = jnp.where(is_odd, w[1][0], w[0][0])
    w_pair = jnp.where(is_odd, w[0][0], w[1][0])
    w_one = jnp.where(is_odd, w[0][1], w[1][1])

    chunks = n // CHUNK
    def x_copy(at, c):
        return remote(g_ref.at[at], x_ref.at[at], x_send, x_recv.at[c], {"energy": pair})

    def one_copy(at, c):
        return remote(g_ref.at[at], one_ref.at[at], one_send, one_recv.at[c], {"energy": one_to})

    def sum_copy(at, c):
        return remote(sum_ref.at[at], got_ref.at[at], sum_send, sum_recv.at[c], {"energy": sum_to})

    def rows_of(c, size=CHUNK):
        return pl.ds(c * size, size)

    def send_one(c):
        at = rows_of(c)
        pl.when(ahead)(lambda: one_copy(at, c * CHUNK // ONE).start())

    def send(c):
        x_copy(rows_of(c), c).start()
        send_one(c)

    th_ref[0], th_ref[1] = th, tl

    def greens(start, rows):
        at = slice(start, start + rows)
        middle = dot3(al[0, at], al[1, at], th_ref[0], th_ref[1])
        g_ref[at] = av[at] + dot3(*split(middle), rr[0], rr[1])

    flipped = list(range(FIRST // CHUNK))
    order = list(range(b // CHUNK, chunks)) + list(range(FIRST // CHUNK, b // CHUNK))
    apart(functools.partial(greens, b, CHUNK))
    send(order[0])
    apart(functools.partial(greens, 0, FIRST))
    for c in flipped:
        raw = remote(g_ref.at[rows_of(c)], got_ref.at[rows_of(c)], sum_send, sum_recv.at[c], {"energy": sum_to})
        pl.when(behind)(raw.start)
        send_one(c)
    apart(functools.partial(greens, b + CHUNK, r - CHUNK))
    for c in order[1:WINDOW]:
        send(c)
    apart(functools.partial(greens, FIRST, b - FIRST))

    def pair_copy(c):
        return remote(pair_ref.at[rows_of(c)], x_ref.at[rows_of(c)], x_send, x_recv.at[c], {"energy": pair})

    def mix(start):
        at = slice(start, start + MIX)
        raw = start < FIRST
        mixed = x_ref[at] if raw else w_pair * x_ref[at]
        mixed = mixed + jnp.where(behind, w_one * one_ref[at], 0.0)
        mixed = mixed + jnp.where(ahead, w_sum_own * got_ref[at] if raw else got_ref[at], 0.0)
        stacked = jnp.concatenate(
            [
                jnp.concatenate([mixed[:, :b], mixed[:, 2 * b : 2 * b + r]], axis=1),
                jnp.concatenate([mixed[:, b : 2 * b], mixed[:, 2 * b + r :]], axis=1),
            ],
            axis=0,
        )
        dressed = dot3(*split(stacked), vt[0], vt[1])
        for i, part in enumerate(split(dressed)):
            q[i, at, :n] = part[:MIX]
            q[i, at, n:] = part[MIX:]
        if start + MIX == n:
            early = slice(b, n)
            acc[...] = dot3(vp[0, :, early], vp[1, :, early], q[0, early], q[1, early])

    seen = set()
    for i in range(chunks + LAG):
        if i < len(order):
            c = order[i]
            x_copy(rows_of(c), c).wait_recv()
            at = slice(c * CHUNK, (c + 1) * CHUNK)
            sum_ref[at] = w_sum_own * g_ref[at] + w_sum_pair * x_ref[at]
            pl.when(behind)(lambda: sum_copy(rows_of(c), c).start())
            later = i + WINDOW
            if later < len(order):
                send(order[later])
            elif later < chunks:
                c = flipped[later - len(order)]
                group = c * CHUNK // ONE
                if group not in seen:
                    seen.add(group)
                    pl.when(behind)(lambda: one_copy(rows_of(group, ONE), group).wait_recv())
                at = slice(c * CHUNK, (c + 1) * CHUNK)
                pair_ref[at] = w_sum_pair * g_ref[at] + jnp.where(behind, w_pair * one_ref[at], 0.0)
                pair_copy(c).start()
        if i >= LAG:
            c = (order + flipped)[i - LAG]
            group = c * CHUNK // ONE
            if group not in seen:
                seen.add(group)
                pl.when(behind)(lambda: one_copy(rows_of(group, ONE), group).wait_recv())
            if c in flipped:
                pair_copy(c).wait_recv()
            pl.when(ahead)(lambda: sum_copy(rows_of(c), c).wait_recv())
            apart(functools.partial(mix, c * CHUNK))
    late = slice(0, b)
    stores = []
    for i in range(2):
        half = slice(i * n, (i + 1) * n)
        res_ref[i] = acc[:, half] + dot3(vp[0, :, late], vp[1, :, late], q[0, late, half], q[1, late, half])
        store = pltpu.make_async_copy(res_ref.at[i], out_ref.at[i, 0, 0], out_sem.at[i])
        store.start()
        stores.append(store)
    every = pl.ds(0, n)
    x_copy(every, 0).wait_send()
    pl.when(ahead)(lambda: one_copy(every, 0).wait_send())
    pl.when(behind)(lambda: sum_copy(every, 0).wait_send())
    for store in stores:
        store.wait()


def per_device(*arrays):
    n = arrays[1].shape[-1]
    b = arrays[2].shape[0]
    chunks = n // CHUNK
    hbm = pl.BlockSpec(memory_space=pl.ANY)
    smem = pl.BlockSpec(memory_space=pltpu.SMEM)
    dma = pltpu.SemaphoreType.DMA
    return pl.pallas_call(
        kernel,
        out_shape=jax.ShapeDtypeStruct(arrays[5].shape, F32),
        in_specs=[hbm] * 7 + [smem] * 2,
        out_specs=hbm,
        scratch_shapes=[
            *(pltpu.VMEM(a.shape, a.dtype) for a in arrays[:7]),
            pltpu.VMEM((2, n, n), F32),
            dma((7,)),
            dma((2,)),
            pltpu.VMEM((2, n, 2 * n), BF16),
            pltpu.VMEM((2, 2 * n, 2 * n), BF16),
            pltpu.VMEM((2, n, 2 * n), BF16),
            pltpu.VMEM((2, 2 * n, 2 * n), BF16),
            pltpu.VMEM((n, 2 * n), F32),
            pltpu.VMEM((2, n, 2 * n), BF16),
            pltpu.VMEM((n, 2 * n), F32),
            pltpu.VMEM((2, n, 2 * b), BF16),
            pltpu.VMEM((2, 2 * b, 2 * n), BF16),
            pltpu.VMEM((2, n, n), BF16),
            pltpu.VMEM((2, n, n), BF16),
            pltpu.VMEM((2, n, 2 * n), BF16),
            pltpu.VMEM((n, 2 * n), F32),
            pltpu.VMEM((2, 2 * b, 2 * b), BF16),
            pltpu.VMEM((2, b, b), F32),
            pltpu.VMEM((b, b), F32),
            pltpu.VMEM((b, b), F32),
            pltpu.VMEM((b, b), F32),
            pltpu.VMEM((2, b, b), F32),
            pltpu.VMEM((n, 2 * n), F32),
            pltpu.VMEM((n, 2 * n), F32),
            pltpu.VMEM((n, 2 * n), F32),
            pltpu.VMEM((n, 2 * n), F32),
            pltpu.VMEM((n, 2 * n), F32),
            pltpu.VMEM((FIRST, 2 * n), F32),
            dma((3,)),
            dma((3,)),
            dma,
            dma((chunks,)),
            dma,
            dma((n // ONE,)),
            dma,
            dma((chunks,)),
        ],
        compiler_params=pltpu.CompilerParams(
            collective_id=0, has_side_effects=True, vmem_limit_bytes=60 * 2**20
        ),
    )(*arrays)


def solution(mesh):
    placed = (
        P("slab", None),
        P("slab", None, None),
        P(),
        P("slab", None),
        P("slab", None),
        P(None, "energy", "slab", None, None),
        P("slab", None, None),
        P(),
        P(),
    )
    return jax.shard_map(
        per_device,
        mesh=mesh,
        in_specs=placed,
        out_specs=P(None, "energy", "slab", None, None),
        check_vma=False,
    )
```

```python
import functools

import jax
import jax.numpy as jnp
from jax import lax
from jax.experimental import pallas as pl
from jax.experimental.pallas import tpu as pltpu
from jax.sharding import PartitionSpec as P

BROADENING = 1.0
LOWEST = -2.0
SPREAD = 4.0
CHUNK = 32
MIX = CHUNK
ONE = 64
WINDOW = 3
LAG = 3
FIRST = 64
F32 = jnp.float32
BF16 = jnp.bfloat16


def split(x):
    high = x.astype(BF16)
    return high, (x - high.astype(F32)).astype(BF16)


def dot(x, y):
    return jnp.dot(x, y, preferred_element_type=F32)


def dot3(xh, xl, yh, yl):
    return dot(jnp.concatenate([xh, xh, xl], axis=1), jnp.concatenate([yh, yl, yh], axis=0))


def rot(p, b):
    r = (p.shape[1] - 2 * b) // 2
    parts = [-p[:, b : 2 * b], p[:, :b]]
    if r:
        parts += [-p[:, 2 * b + r :], p[:, 2 * b : 2 * b + r]]
    return jnp.concatenate(parts, axis=1)


def rot_rest(p):
    r = p.shape[1] // 2
    return jnp.concatenate([-p[:, r:], p[:, :r]], axis=1)


def iota(shape, axis):
    return lax.broadcasted_iota(jnp.int32, shape, axis)


def kernel(
    onsite_in,
    hop_in,
    ham_in,
    cpl_in,
    bound_in,
    sigma_in,
    vertex_in,
    steps_ref,
    weights_ref,
    out_ref,
    onsite_ref,
    hop_ref,
    ham_ref,
    cpl_ref,
    bound_ref,
    sigma_ref,
    vertex_ref,
    res_ref,
    in_sem,
    out_sem,
    khl,
    rhs,
    k2l,
    k4r,
    yv,
    yl,
    av,
    al,
    rr,
    vp,
    vt,
    q,
    acc,
    th_ref,
    s_ref,
    r1_ref,
    h2_ref,
    r2_ref,
    f_ref,
    g_ref,
    x_ref,
    one_ref,
    sum_ref,
    got_ref,
    pair_ref,
    schur_send,
    schur_recv,
    x_send,
    x_recv,
    one_send,
    one_recv,
    sum_send,
    sum_recv,
):
    n = hop_ref.shape[-1]
    b = ham_ref.shape[0]
    r = n - b
    slab = lax.axis_index("slab")
    e = lax.axis_index("energy")
    energies = lax.axis_size("energy")
    core = lax.rem(slab, 2)
    other_core = slab + 1 - 2 * core
    other_chip = lax.rem(slab + 2, 4)
    odd = lax.rem(e, 2)
    pair = e + 1 - 2 * odd
    one_to = e - 2 + 4 * odd
    sum_to = e + 2 - 4 * odd
    ahead = (one_to >= 0) & (one_to < energies)
    behind = (sum_to >= 0) & (sum_to < energies)
    one_to = lax.rem(one_to + energies, energies)
    sum_to = lax.rem(sum_to + energies, energies)

    loads = [
        pltpu.make_async_copy(src, dst, in_sem.at[i])
        for i, (src, dst) in enumerate(
            (
                (bound_in, bound_ref),
                (sigma_in, sigma_ref),
                (hop_in, hop_ref),
                (onsite_in, onsite_ref),
                (cpl_in, cpl_ref),
                (ham_in, ham_ref),
                (vertex_in, vertex_ref),
            )
        )
    ]
    for load in loads[:5]:
        load.start()
    barrier = pltpu.get_barrier_semaphore()

    def greet(target):
        pl.semaphore_signal(barrier, inc=1, device_id=target, device_id_type=pl.DeviceIdType.MESH)

    greet({"slab": other_core})
    greet({"slab": other_chip})
    greet({"energy": pair})
    pl.when(ahead)(lambda: greet({"energy": one_to}))
    pl.when(behind)(lambda: greet({"energy": sum_to}))

    def remote(src, dst, send, recv, target):
        return pltpu.make_async_remote_copy(
            src_ref=src,
            dst_ref=dst,
            send_sem=send,
            recv_sem=recv,
            device_id=target,
            device_id_type=pl.DeviceIdType.MESH,
        )

    def apart(work):
        pl.when(slab >= 0)(work)

    energy_value = LOWEST + SPREAD * (e.astype(F32) + 0.5) / energies

    loads[0].wait()
    eye_b = iota((b, b), 0) == iota((b, b), 1)
    bound_row = bound_ref[...]
    bound_col = jnp.sum(jnp.where(eye_b, bound_row, 0), axis=1, keepdims=True)
    here = iota((b, n), 1)
    count = jnp.sum(jnp.where(bound_col < here, 1, 0), axis=0, keepdims=True)
    is_bound = jnp.sum(jnp.where(bound_col == here, 1, 0), axis=0, keepdims=True)
    at = iota((1, n), 1)
    pos_row = jnp.where(is_bound > 0, count, b + at - count)
    here = iota((n, b), 0)
    count = jnp.sum(jnp.where(bound_row < here, 1, 0), axis=1, keepdims=True)
    is_bound = jnp.sum(jnp.where(bound_row == here, 1, 0), axis=1, keepdims=True)
    at = iota((n, 1), 0)
    pos_col = jnp.where(is_bound > 0, count, b + at - count)
    perm_mask = iota((n, n), 0) == pos_row
    perm = jnp.where(perm_mask, 1.0, 0.0).astype(BF16)
    perm_t = jnp.where(iota((n, n), 1) == pos_col, 1.0, 0.0).astype(BF16)

    for load in loads[1:4]:
        load.wait()
    for load in loads[5:]:
        load.start()
    eye = iota((n, n), 0) == iota((n, n), 1)
    sr = hop_ref[0] + sigma_ref[0, 0, 0]
    si = sigma_ref[1, 0, 0]
    dr = energy_value - onsite_ref[...] - jnp.sum(jnp.where(eye, sr, 0.0), axis=0, keepdims=True)
    di = BROADENING - jnp.sum(jnp.where(eye, si, 0.0), axis=0, keepdims=True)
    magnitude = dr * dr + di * di
    dr, di = dr / magnitude, -di / magnitude
    nr = jnp.where(eye, 0.0, -sr)
    ni = jnp.where(eye, 0.0, -si)
    krh, krl = split(nr * dr - ni * di)
    kih, kil = split(nr * di + ni * dr)
    moved = dot(perm, jnp.concatenate([krh, kih, krl, kil], axis=1)).astype(BF16)
    moved = jnp.concatenate([moved[:, i * n : (i + 1) * n] for i in range(4)], axis=0)
    moved = dot(moved, perm_t).astype(BF16)
    krh, kih, krl, kil = (moved[i * n : (i + 1) * n] for i in range(4))
    rows = iota((8, n), 0)
    pieces = jnp.zeros((8, n), F32)
    for i, d in enumerate((dr, di)):
        for j in range(3):
            part = d.astype(BF16).astype(F32)
            pieces = jnp.where(rows == 3 * i + j, part, pieces)
            d = d - part
    pieces = dot(pieces.astype(BF16), perm_t).T
    dr_col = pieces[:, 0:1] + pieces[:, 1:2] + pieces[:, 2:3]
    di_col = pieces[:, 3:4] + pieces[:, 4:5] + pieces[:, 5:6]

    def ordered(re, im):
        return jnp.concatenate([re[:, :b], im[:, :b], re[:, b:], im[:, b:]], axis=1)

    def store_rhs(ref, at, p, turned, columns):
        ref[at, 0:b, columns] = p[:b]
        ref[at, b : 2 * b, columns] = turned[:b]
        ref[at, 2 * b : 2 * b + r, columns] = p[b:]
        ref[at, 2 * b + r :, columns] = turned[b:]

    whole = slice(0, 2 * n)
    first = slice(0, 2 * b)
    rest = slice(2 * b, 2 * n)
    for i, p in enumerate((ordered(krh, kih), ordered(krl, kil))):
        khl[i] = p
        store_rhs(rhs, i, p, rot(p, b), whole)

    p = dot3(khl[0], khl[1], rhs[0], rhs[1])
    yv[...] = p
    for i, part in enumerate(split(p)):
        k2l[i] = part
        store_rhs(rhs, i, part, rot(part, b), whole)

    def identity(start, rows):
        row = iota((rows, 2 * n), 0) + start
        column = iota((rows, 2 * n), 1)
        orbital = jnp.where(column < b, column, jnp.where((column >= 2 * b) & (column < 2 * b + r), column - b, -1))
        return jnp.where(row == orbital, 1.0, 0.0)

    def y_rows(start, rows, k3=None):
        at = slice(start, start + rows)
        if k3 is None:
            k3 = dot3(khl[0, at], khl[1, at], rhs[0], rhs[1])
        u = identity(start, rows) - khl[0, at].astype(F32) - khl[1, at].astype(F32) + yv[at] - k3
        y = dr_col[at] * u + di_col[at] * rot(u, b)
        yv[at] = y
        for i, part in enumerate(split(y)):
            yl[i, at] = part

    def k4_columns(columns, turn):
        p = dot3(k2l[0], k2l[1], rhs[0, :, columns], rhs[1, :, columns])
        for i, part in enumerate(split(p)):
            store_rhs(k4r, i, part, turn(part), columns)

    stacked = [jnp.concatenate([khl[i, :b], k2l[i]], axis=0) for i in range(2)]
    stacked = dot3(*stacked, rhs[0, :, first], rhs[1, :, first])
    for i, part in enumerate(split(stacked[b:])):
        store_rhs(k4r, i, part, rot(part, b), first)
    k3 = dot3(khl[0, :b], khl[1, :b], rhs[0, :, rest], rhs[1, :, rest])
    y_rows(0, b, jnp.concatenate([stacked[:b], k3], axis=1))
    corner = yv[:b, first] + dot3(yl[0, :b], yl[1, :b], k4r[0, :, first], k4r[1, :, first])
    loads[4].wait()
    c_row = cpl_ref[...]
    c_col = jnp.sum(jnp.where(eye_b, c_row, 0.0), axis=1, keepdims=True)
    c_both = c_col * c_row
    s_ref[0] = corner[:, :b] * c_both
    s_ref[1] = corner[:, b:] * c_both

    pl.semaphore_wait(barrier, 3 + ahead.astype(jnp.int32) + behind.astype(jnp.int32))
    step1 = remote(s_ref.at[1 - core], r1_ref, schur_send.at[0], schur_recv.at[0], {"slab": other_core})
    step1.start()
    @apart
    def _():
        k4_columns(rest, rot_rest)

    step1.wait()
    h2_ref[...] = s_ref[core] + r1_ref[...]
    step2 = remote(h2_ref, r2_ref, schur_send.at[1], schur_recv.at[1], {"slab": other_chip})
    step2.start()

    def finish_inverse():
        y_rows(b, r)
        a = yv[...] + dot3(yl[0], yl[1], k4r[0], k4r[1])
        av[...] = a
        for i, part in enumerate(split(a[:, first])):
            al[i] = part
        for i, part in enumerate(split(a[:b])):
            rr[i, :b] = part
            rr[i, b:] = rot(part, b)

    apart(finish_inverse)

    step2.wait()
    f_ref[core] = h2_ref[...] + r2_ref[...]
    step3 = remote(f_ref.at[core], f_ref.at[core], schur_send.at[2], schur_recv.at[2], {"slab": other_core})
    step3.start()
    loads[5].wait()
    loads[6].wait()

    def order_vertex():
        for i, part in enumerate(split(vertex_ref[0])):
            v = dot(part, perm_t)
            vp[i] = v.astype(BF16)
            vt[i] = v.T.astype(BF16)

    apart(order_vertex)
    step3.wait()

    tr = jnp.where(eye_b, 0.0, -ham_ref[...] - f_ref[0])
    ti = jnp.where(eye_b, 0.0, -f_ref[1])
    diag_r = jnp.where(eye_b, energy_value - ham_ref[...] - f_ref[0], 0.0)
    diag_i = jnp.where(eye_b, BROADENING - f_ref[1], 0.0)

    def reciprocal(axis):
        zr = jnp.sum(diag_r, axis=axis, keepdims=True)
        zi = jnp.sum(diag_i, axis=axis, keepdims=True)
        size = zr * zr + zi * zi
        return zr / size, -zi / size

    er, ei = reciprocal(0)
    er_col, ei_col = reciprocal(1)
    k = jnp.concatenate([tr * er - ti * ei, tr * ei + ti * er], axis=1)

    def turned(parts):
        return [jnp.concatenate([part, rot(part, b)], axis=0) for part in parts]

    one = jnp.where(iota((b, 2 * b), 0) == iota((b, 2 * b), 1), 1.0, 0.0)
    kl = split(k)
    k2 = dot3(*kl, *turned(kl))
    k2s = split(k2)
    k2t = turned(k2s)
    both = dot3(*(jnp.concatenate(pieces, axis=0) for pieces in zip(kl, k2s)), *k2t)
    k3, k4 = both[:b], both[b:]
    u = one - k + k2 - k3
    u = er_col * u + ei_col * rot(u, b)
    t = u + dot3(*split(u), *turned(split(k4)))
    t = t * jnp.concatenate([c_both, c_both], axis=1)
    th, tl = turned(split(t))

    w = [[jnp.float32(0.0), jnp.float32(0.0)], [jnp.float32(0.0), jnp.float32(0.0)]]
    for way in range(2):
        for d in range(2):
            for m in range(2):
                w[way][d] = w[way][d] + jnp.where(steps_ref[m] == d + 1, weights_ref[way, m], 0.0)
    is_odd = odd == 1
    w_sum_own = jnp.where(is_odd, w[1][1], w[0][1])
    w_sum_pair = jnp.where(is_odd, w[1][0], w[0][0])
    w_pair = jnp.where(is_odd, w[0][0], w[1][0])
    w_one = jnp.where(is_odd, w[0][1], w[1][1])

    chunks = n // CHUNK
    def x_copy(at, c):
        return remote(g_ref.at[at], x_ref.at[at], x_send, x_recv.at[c], {"energy": pair})

    def one_copy(at, c):
        return remote(g_ref.at[at], one_ref.at[at], one_send, one_recv.at[c], {"energy": one_to})

    def sum_copy(at, c):
        return remote(sum_ref.at[at], got_ref.at[at], sum_send, sum_recv.at[c], {"energy": sum_to})

    def rows_of(c, size=CHUNK):
        return pl.ds(c * size, size)

    def send_one(c):
        at = rows_of(c)
        pl.when(ahead)(lambda: one_copy(at, c * CHUNK // ONE).start())

    def send(c):
        x_copy(rows_of(c), c).start()
        send_one(c)

    th_ref[0], th_ref[1] = th, tl

    def greens(start, rows):
        at = slice(start, start + rows)
        middle = dot3(al[0, at], al[1, at], th_ref[0], th_ref[1])
        g_ref[at] = av[at] + dot3(*split(middle), rr[0], rr[1])

    flipped = list(range(FIRST // CHUNK))
    order = list(range(b // CHUNK, chunks)) + list(range(FIRST // CHUNK, b // CHUNK))
    apart(functools.partial(greens, b, CHUNK))
    send(order[0])
    apart(functools.partial(greens, 0, FIRST))
    for c in flipped:
        raw = remote(g_ref.at[rows_of(c)], got_ref.at[rows_of(c)], sum_send, sum_recv.at[c], {"energy": sum_to})
        pl.when(behind)(raw.start)
        send_one(c)
    apart(functools.partial(greens, b + CHUNK, r - CHUNK))
    for c in order[1:WINDOW]:
        send(c)
    apart(functools.partial(greens, FIRST, b - FIRST))

    def pair_copy(c):
        return remote(pair_ref.at[rows_of(c)], x_ref.at[rows_of(c)], x_send, x_recv.at[c], {"energy": pair})

    def mix(start):
        at = slice(start, start + MIX)
        raw = start < FIRST
        mixed = x_ref[at] if raw else w_pair * x_ref[at]
        mixed = mixed + jnp.where(behind, w_one * one_ref[at], 0.0)
        mixed = mixed + jnp.where(ahead, w_sum_own * got_ref[at] if raw else got_ref[at], 0.0)
        stacked = jnp.concatenate(
            [
                jnp.concatenate([mixed[:, :b], mixed[:, 2 * b : 2 * b + r]], axis=1),
                jnp.concatenate([mixed[:, b : 2 * b], mixed[:, 2 * b + r :]], axis=1),
            ],
            axis=0,
        )
        dressed = dot3(*split(stacked), vt[0], vt[1])
        for i, part in enumerate(split(dressed)):
            q[i, at, :n] = part[:MIX]
            q[i, at, n:] = part[MIX:]
        if start + MIX == n:
            early = slice(b, n)
            acc[...] = dot3(vp[0, :, early], vp[1, :, early], q[0, early], q[1, early])

    seen = set()
    for i in range(chunks + LAG):
        if i < len(order):
            c = order[i]
            x_copy(rows_of(c), c).wait_recv()
            at = slice(c * CHUNK, (c + 1) * CHUNK)
            sum_ref[at] = w_sum_own * g_ref[at] + w_sum_pair * x_ref[at]
            pl.when(behind)(lambda: sum_copy(rows_of(c), c).start())
            later = i + WINDOW
            if later < len(order):
                send(order[later])
            elif later < chunks:
                c = flipped[later - len(order)]
                group = c * CHUNK // ONE
                if group not in seen:
                    seen.add(group)
                    pl.when(behind)(lambda: one_copy(rows_of(group, ONE), group).wait_recv())
                at = slice(c * CHUNK, (c + 1) * CHUNK)
                pair_ref[at] = w_sum_pair * g_ref[at] + jnp.where(behind, w_pair * one_ref[at], 0.0)
                pair_copy(c).start()
        if i >= LAG:
            c = (order + flipped)[i - LAG]
            group = c * CHUNK // ONE
            if group not in seen:
                seen.add(group)
                pl.when(behind)(lambda: one_copy(rows_of(group, ONE), group).wait_recv())
            if c in flipped:
                pair_copy(c).wait_recv()
            pl.when(ahead)(lambda: sum_copy(rows_of(c), c).wait_recv())
            apart(functools.partial(mix, c * CHUNK))
    late = slice(0, b)
    stores = []
    for i in range(2):
        half = slice(i * n, (i + 1) * n)
        res_ref[i] = acc[:, half] + dot3(vp[0, :, late], vp[1, :, late], q[0, late, half], q[1, late, half])
        store = pltpu.make_async_copy(res_ref.at[i], out_ref.at[i, 0, 0], out_sem.at[i])
        store.start()
        stores.append(store)
    every = pl.ds(0, n)
    x_copy(every, 0).wait_send()
    pl.when(ahead)(lambda: one_copy(every, 0).wait_send())
    pl.when(behind)(lambda: sum_copy(every, 0).wait_send())
    for store in stores:
        store.wait()


def per_device(*arrays):
    n = arrays[1].shape[-1]
    b = arrays[2].shape[0]
    chunks = n // CHUNK
    hbm = pl.BlockSpec(memory_space=pl.ANY)
    smem = pl.BlockSpec(memory_space=pltpu.SMEM)
    dma = pltpu.SemaphoreType.DMA
    return pl.pallas_call(
        kernel,
        out_shape=jax.ShapeDtypeStruct(arrays[5].shape, F32),
        in_specs=[hbm] * 7 + [smem] * 2,
        out_specs=hbm,
        scratch_shapes=[
            *(pltpu.VMEM(a.shape, a.dtype) for a in arrays[:7]),
            pltpu.VMEM((2, n, n), F32),
            dma((7,)),
            dma((2,)),
            pltpu.VMEM((2, n, 2 * n), BF16),
            pltpu.VMEM((2, 2 * n, 2 * n), BF16),
            pltpu.VMEM((2, n, 2 * n), BF16),
            pltpu.VMEM((2, 2 * n, 2 * n), BF16),
            pltpu.VMEM((n, 2 * n), F32),
            pltpu.VMEM((2, n, 2 * n), BF16),
            pltpu.VMEM((n, 2 * n), F32),
            pltpu.VMEM((2, n, 2 * b), BF16),
            pltpu.VMEM((2, 2 * b, 2 * n), BF16),
            pltpu.VMEM((2, n, n), BF16),
            pltpu.VMEM((2, n, n), BF16),
            pltpu.VMEM((2, n, 2 * n), BF16),
            pltpu.VMEM((n, 2 * n), F32),
            pltpu.VMEM((2, 2 * b, 2 * b), BF16),
            pltpu.VMEM((2, b, b), F32),
            pltpu.VMEM((b, b), F32),
            pltpu.VMEM((b, b), F32),
            pltpu.VMEM((b, b), F32),
            pltpu.VMEM((2, b, b), F32),
            pltpu.VMEM((n, 2 * n), F32),
            pltpu.VMEM((n, 2 * n), F32),
            pltpu.VMEM((n, 2 * n), F32),
            pltpu.VMEM((n, 2 * n), F32),
            pltpu.VMEM((n, 2 * n), F32),
            pltpu.VMEM((FIRST, 2 * n), F32),
            dma((3,)),
            dma((3,)),
            dma,
            dma((chunks,)),
            dma,
            dma((n // ONE,)),
            dma,
            dma((chunks,)),
        ],
        compiler_params=pltpu.CompilerParams(
            collective_id=0, has_side_effects=True, vmem_limit_bytes=60 * 2**20
        ),
    )(*arrays)


def solution(mesh):
    placed = (
        P("slab", None),
        P("slab", None, None),
        P(),
        P("slab", None),
        P("slab", None),
        P(None, "energy", "slab", None, None),
        P("slab", None, None),
        P(),
        P(),
    )
    return jax.shard_map(
        per_device,
        mesh=mesh,
        in_specs=placed,
        out_specs=P(None, "energy", "slab", None, None),
        check_vma=False,
    )
```
